32 devices in a mesh: groups: 2 (over y), wide: 4 (over x, core), narrow: 4 (over z).
Axes of the slice: x: 2, y: 2, z: 4, core: 2. Of those that a mesh axis runs over, the one named last changes fastest.
Arguments:
- spectra: bfloat16 [2, 32, 640, 2, 1281], P(None, ('groups', 'wide'), 'narrow'), parts along dimension 1, may hold values from -6 to 6
- legendre: bfloat16 [320, 1281, 128], P('narrow'), may hold values from -0.15625 to 0.15625
- pair_of_slot: int32 [640], replicated, may hold values from 0 to 639, each once
- lat_owner: int32 [128], replicated, may hold values from 0 to 3, as said below
- region_of_lon: int32 [2048], replicated, may hold values from 0 to 63, never falling along the last dimension, each value on 1 to 48 neighbouring positions
Outputs:
- peak: float32 [4, 128, 64], P('groups', 'narrow', 'wide'), parts along dimension 0
- peak_slope: float32 [4, 128, 64], P('groups', 'narrow', 'wide'), parts along dimension 0
The draws below stay inside these ranges and needn't reach their ends.
There are 2 independent parts, one for each index of `groups`. The reference program is written for one: setup_inputs(seed, part) draws one part's arguments, and reference() takes and returns one part's arrays. A program takes and returns all parts, laid end to end along the dimension named above; an argument that names none is the same for every part. Nothing has to cross between parts.
Inputs may be any that keep to these rules, and one draw needn't show every extreme that they name: `lat_owner`: each index of narrow owns exactly 32 latitudes. `region_of_lon`: regions never fall along the longitudes and every region has at least one longitude. `pair_of_slot`: a permutation.
All inputs are finite; a program needn't handle non-finite values.
Results may differ from the reference program's by a relative error of at most 0.0003.
Values sent between devices are 32-bit elements; how exact they have to be, the bound alone decides.
No kernel may reach another device: no remote copies, remote signals or barrier semaphores. Data moves between devices by JAX's collectives and lax.ppermute only.
A program may use at most 192 MiB of HBM per device.

```python
import math
import jax
import jax.numpy as jnp
import numpy as np
from jax import lax

M = 1280
LAT = 128
LON = 2048
MEMBERS = 2
PAIRS = 640
PAIR_LEN = 1281
LATH = 64
LAT_DEV = 32
LON_FULL = 5120
TIMES = 16
REGIONS = 64


def draw_lat_owner(key, part):
    shuffled = jax.random.permutation(key, LAT)
    return (shuffled // LAT_DEV).astype(jnp.int32)


def shard_levels(rng, dims, split, least, largest):
    factor_of = 1.0
    for axis_at, parts in split:
        steps = jax.random.uniform(jax.random.fold_in(jax.random.fold_in(rng, 6), axis_at), (parts,), jnp.float32, least / len(split), largest / len(split))
        factor_of = factor_of * jnp.repeat(jnp.exp(steps), dims[axis_at] // parts).reshape((-1,) + (1,) * (len(dims) - 1 - axis_at))
    return factor_of


def split_up(number_of, total, bound, skew):
    loads = [(1 << 20) // math.isqrt(rank ** skew) + 1 for rank in range(2, number_of + 1)]
    surplus, given = total - bound - (number_of - 1), [1] * (number_of - 1)
    while surplus > 0:
        movable = [i for i in range(number_of - 1) if given[i] < bound]
        whole, budget = sum([loads[i] for i in movable]), surplus
        for i in movable:
            extra = min(bound - given[i], max(1, budget * loads[i] // whole), surplus)
            given[i] = given[i] + extra
            surplus = surplus - extra
    return np.array([bound] + given)


def ragged(own_key, number_of, total, most, skew):
    if number_of == 2:
        one = jax.random.randint(own_key, (), max(1, total - most), min(most, total - 1) + 1)
        return jnp.stack([one, total - one])
    tallies = jnp.asarray(split_up(number_of, total, most, skew), jnp.int32)
    twos = (number_of - 1) // 2
    source_of, taker = tallies[1:1 + 2 * twos:2], tallies[2:2 + 2 * twos:2]
    room = jnp.minimum(source_of - 1, most - taker)
    shifted = jax.random.randint(jax.random.fold_in(own_key, 1), (twos,), 0, 1 << 20) % (room + 1)
    tallies = tallies.at[1:1 + 2 * twos:2].set(source_of - shifted).at[2:2 + 2 * twos:2].set(taker + shifted)
    return tallies[jax.random.permutation(jax.random.fold_in(own_key, 2), number_of)]


def scatter_about(key, extent, spread, bound, cuts=(), held_as=jnp.bfloat16):
    drawn = spread * jax.random.normal(key, extent, jnp.float32)
    if cuts:
        drawn = drawn * shard_levels(key, extent, cuts, -0.22, 0.18)
    return jnp.clip(drawn, -bound, bound).astype(held_as)


def setup_inputs(seed: int = 0, part: int = 0) -> dict:
    streams_of = jax.random.split(jax.random.key(seed), 6)
    part_keys = jax.random.split(jax.random.fold_in(streams_of[5], part), 6)
    return {
        "spectra": scatter_about(part_keys[0], (MEMBERS, TIMES, PAIRS, 2, PAIR_LEN), 1.0, 6.0, ((1, 4), (2, 4))),
        "legendre": scatter_about(streams_of[1], (PAIRS // 2, PAIR_LEN, 2 * LATH), M ** -0.5, 0.15625, ((0, 4),)),
        "pair_of_slot": jax.random.permutation(streams_of[2], PAIRS).astype(jnp.int32),
        "lat_owner": draw_lat_owner(jax.random.fold_in(streams_of[5], 71), part),
        "region_of_lon": jnp.searchsorted(jnp.cumsum(ragged(streams_of[4], REGIONS, LON, 48, 0)), jnp.arange(LON), side="right").astype(jnp.int32),
    }


def legendre_slot(coef, table, paired):
    position = jnp.arange(PAIR_LEN, dtype=jnp.int32)
    first_len = M - paired
    leading = position < first_len
    offset = jnp.where(leading, position, position - first_len)
    even_term = offset % 2 == 0
    masks = jnp.stack([leading & even_term, leading & ~even_term, ~leading & even_term, ~leading & ~even_term], axis=0).astype(jnp.float32)
    masked = masks[:, None, None, None, :] * coef.astype(jnp.float32)[None]
    sums = jnp.einsum("getcl,lj->getcj", masked, table.astype(jnp.float32), precision=lax.Precision.HIGHEST)
    north_lead = sums[0] + sums[1]
    south_lead = sums[0] - sums[1]
    north_tail = sums[2] + sums[3]
    south_tail = sums[2] - sums[3]
    lead = jnp.concatenate([north_lead, jnp.flip(south_lead, axis=-1)], axis=-1)
    tail = jnp.concatenate([north_tail, jnp.flip(south_tail, axis=-1)], axis=-1)
    return jnp.stack([lead, tail], axis=0)


def synthesize(operand, waves, start, width):
    columns = start + jnp.arange(width, dtype=jnp.int32)
    phase = (waves[:, None] * columns[None, :]) % LON_FULL
    angle = phase.astype(jnp.float32) * (2.0 * math.pi / LON_FULL)
    cosine = jnp.cos(angle)
    sine = jnp.sin(angle)
    rate = (waves.astype(jnp.float32) / M)[:, None]
    upper = jnp.concatenate([cosine, -rate * sine], axis=1)
    lower = jnp.concatenate([-sine, -rate * cosine], axis=1)
    table = jnp.concatenate([upper, lower], axis=0) * (M ** -0.5)
    return jnp.dot(operand, table, precision=lax.Precision.HIGHEST)


def synthesize_all(operand, waves):
    width = min(512, LON)
    starts = jnp.arange(LON // width, dtype=jnp.int32) * width

    def one_block(begin):
        return synthesize(operand, waves, begin, width)

    blocks = lax.map(one_block, starts)
    blocks = blocks.reshape(blocks.shape[0], blocks.shape[1], 2, width)
    value = jnp.transpose(blocks[:, :, 0], (1, 0, 2)).reshape(operand.shape[0], LON)
    slope = jnp.transpose(blocks[:, :, 1], (1, 0, 2)).reshape(operand.shape[0], LON)
    return value, slope


def region_peak(values, region_of_lon, wanted):
    hits = region_of_lon[:, None] == wanted[None, :]
    masked = jnp.where(hits[None, None], values[..., None], -1e30)
    return masked.max(axis=2)


def reference(spectra, legendre, pair_of_slot, lat_owner, region_of_lon):
    table_all = legendre.reshape(PAIRS // 2, PAIR_LEN, 2, LATH)
    table_all = jnp.transpose(table_all, (0, 2, 1, 3)).reshape(PAIRS, PAIR_LEN, LATH)

    def per_slot(items):
        return legendre_slot(items[0], items[1], items[2])

    slotted = lax.map(per_slot, (jnp.moveaxis(spectra, 2, 0), table_all, pair_of_slot))
    grid = jnp.zeros((M, MEMBERS, TIMES, 2, LAT), jnp.float32)
    grid = grid.at[pair_of_slot].set(slotted[:, 0])
    grid = grid.at[M - 1 - pair_of_slot].set(slotted[:, 1])
    order = jnp.argsort(lat_owner, stable=True).astype(jnp.int32)
    grid = jnp.take(grid, order, axis=4)
    operand = jnp.transpose(grid, (1, 2, 4, 3, 0)).reshape(MEMBERS * TIMES * LAT, 2 * M)
    waves = jnp.arange(M, dtype=jnp.int32)
    value, slope = synthesize_all(operand, waves)
    value = value.reshape(MEMBERS, TIMES, LAT, LON).max(axis=1)
    slope = jnp.abs(slope).reshape(MEMBERS, TIMES, LAT, LON).max(axis=1)
    wanted = jnp.arange(REGIONS, dtype=jnp.int32)
    peak = region_peak(value, region_of_lon, wanted)
    peak_slope = region_peak(slope, region_of_lon, wanted)
    return peak, peak_slope
```

```python
import functools
import math

import jax
import jax.numpy as jnp
from jax import lax
from jax.experimental import pallas as pl
from jax.experimental.pallas import tpu as pltpu
from jax.sharding import PartitionSpec as P

REG_DEV = 16
WIDEST_REGION = 48
LANES = 128
PAIRS_UNIT = 8
NB = 32
VMEM = 56 * 2**20
CHUNKS = (1, 2, 3, 2, 2)
STAGES = ((0, 1, 2), (3,), (4,))
F32 = jnp.float32
BF16 = jnp.bfloat16


def synthesize(operand, waves, start, width, top):
    columns = start + jnp.arange(width, dtype=jnp.int32)
    phase = waves[:, None] * columns[None, :] % (4 * top)
    angle = phase.astype(F32) * (2.0 * math.pi / (4 * top))
    cosine = jnp.cos(angle)
    sine = jnp.sin(angle)
    rate = (waves.astype(F32) / top)[:, None]
    upper = jnp.concatenate([cosine, -rate * sine], axis=1)
    lower = jnp.concatenate([-sine, -rate * cosine], axis=1)
    table = jnp.concatenate([upper, lower], axis=0) * top ** (-0.5)
    return jnp.dot(operand, table, precision=lax.Precision.HIGHEST)


def synthesize_all(operand, waves, lon, top):
    width = min(512, lon)
    starts = jnp.arange(lon // width, dtype=jnp.int32) * width
    blocks = lax.map(lambda begin: synthesize(operand, waves, begin, width, top), starts)
    blocks = blocks.reshape(blocks.shape[0], blocks.shape[1], 2, width)
    value = jnp.transpose(blocks[:, :, 0], (1, 0, 2)).reshape(operand.shape[0], lon)
    slope = jnp.transpose(blocks[:, :, 1], (1, 0, 2)).reshape(operand.shape[0], lon)
    return value, slope


def region_peak(values, region_of_lon, wanted):
    hits = region_of_lon[:, None] == wanted[None, :]
    masked = jnp.where(hits[None, None], values[..., None], -1e30)
    return masked.max(axis=2)


def plain(spectra, legendre, pair_of_slot, lat_owner, region_of_lon):
    members, steps_here, slot_count, _, length = spectra.shape
    top = length - 1
    lon = region_of_lon.shape[0]
    half_count = legendre.shape[0]
    lat_half = legendre.shape[2] // 2
    here = lax.axis_index("narrow")
    paired = lax.dynamic_slice_in_dim(pair_of_slot, here * slot_count, slot_count)
    position = jnp.arange(length, dtype=jnp.int32)[None, :]
    first_len = (top - paired)[:, None]
    leading = position < first_len
    offset = jnp.where(leading, position, position - first_len)
    even_term = offset % 2 == 0
    masks = jnp.stack(
        [leading & even_term, leading & ~even_term, ~leading & even_term, ~leading & ~even_term],
        axis=1,
    ).astype(BF16)
    ordered = jnp.transpose(spectra, (2, 0, 1, 3, 4))
    masked = masks[:, :, None, None, None, :] * ordered[:, None]
    masked = masked.reshape(half_count, 2, -1, length)
    table = legendre.reshape(half_count, length, 2, lat_half)
    sums = jnp.einsum("abrl,albj->abrj", masked, table, preferred_element_type=F32)
    sums = sums.reshape(slot_count, 4, members, steps_here, 2, lat_half)
    north_lead = sums[:, 0] + sums[:, 1]
    south_lead = sums[:, 0] - sums[:, 1]
    north_tail = sums[:, 2] + sums[:, 3]
    south_tail = sums[:, 2] - sums[:, 3]
    lead = jnp.concatenate([north_lead, jnp.flip(south_lead, axis=-1)], axis=-1)
    tail = jnp.concatenate([north_tail, jnp.flip(south_tail, axis=-1)], axis=-1)
    waved = jnp.stack([lead, tail], axis=1).reshape(2 * slot_count, members, steps_here, 2, -1)
    order = jnp.argsort(lat_owner, stable=True)
    waved = jnp.take(waved, order, axis=4)
    arrived = lax.all_to_all(waved, "narrow", split_axis=4, concat_axis=0, tiled=True)
    waves = jnp.stack([pair_of_slot, top - 1 - pair_of_slot], axis=1).reshape(-1)
    lat_here = arrived.shape[4]
    operand = jnp.transpose(arrived, (1, 2, 4, 3, 0)).reshape(members * steps_here * lat_here, -1)
    value, slope = synthesize_all(operand, waves, lon, top)
    value = value.reshape(members, steps_here, lat_here, lon).max(axis=1)
    slope = jnp.abs(slope).reshape(members, steps_here, lat_here, lon).max(axis=1)
    wide_count = lax.axis_size("wide")
    mine_start = lax.axis_index("wide") * REG_DEV
    wanted = jnp.arange(REG_DEV * wide_count, dtype=jnp.int32)
    peaks = region_peak(value, region_of_lon, wanted)
    slopes = region_peak(slope, region_of_lon, wanted)
    peaks, slopes = lax.pmax((peaks, slopes), "wide")
    peak = lax.dynamic_slice_in_dim(peaks, mine_start, REG_DEV, 2)
    peak_slope = lax.dynamic_slice_in_dim(slopes, mine_start, REG_DEV, 2)
    return peak, peak_slope


def iota(shape, axis):
    return lax.broadcasted_iota(jnp.int32, shape, axis)


def latitude_lanes(owner, here, parts):
    square = (LANES, LANES)
    row = jnp.broadcast_to(owner.astype(F32), square)
    column = row.T
    first, second = iota(square, 0), iota(square, 1)
    ahead = (column < row) | ((column == row) & (first < second))
    place = jnp.sum(jnp.where(ahead, 1.0, 0.0), axis=0, keepdims=True)
    place = jnp.broadcast_to(place, square).T
    half = LANES // 2
    lane_of = jnp.where(first < half, first, half + LANES - 1 - first).astype(F32)
    share = LANES // parts
    rows = []
    for step in range(parts):
        owner_index = lax.rem(here + step, parts)
        target = (owner_index * share + second % share).astype(F32)
        rows.append(jnp.sum(jnp.where(place == target, lane_of, 0.0), axis=0, keepdims=True))
    return jnp.concatenate(rows, axis=0).astype(jnp.int32)


def legendre_kernel(first_unit, parts, pair_ref, here_ref, owner_ref, s_ref, l_ref, *refs):
    outs, (lanes_ref, table, sums) = refs[:parts], refs[parts:]
    members, steps, slots, _, length = s_ref.shape
    top = length - 1
    times = members * steps
    rows = 2 * times
    unit = pl.program_id(0)
    here = here_ref[0]

    @pl.when(unit == 0)
    def _():
        lanes_ref[...] = latitude_lanes(owner_ref[...], here, parts)

    def turn(i, carry):
        at = pl.multiple_of(i * LANES, LANES)
        table[:, pl.ds(at, LANES), :] = jnp.swapaxes(l_ref[pl.ds(at, LANES)], 0, 1)
        return carry

    lax.fori_loop(0, top // LANES, turn, 0)

    spot = iota((rows, top), 1)
    even = jnp.where(spot % 2 == 0, 1.0, 0.0).astype(BF16)
    base = (here * pl.num_programs(0) * 0) + here * (pair_ref.shape[0] // parts) + (first_unit + unit) * slots
    low = iota((rows, LANES), 1) < LANES // 2
    for pair in range(slots // 2):
        parts_of, last, signs = [], [], []
        for side in range(2):
            slot = 2 * pair + side
            whole = s_ref[:, :, slot].reshape(rows, length)
            x = whole[:, :top]
            last.append(whole[:, top:].astype(F32))
            first_len = top - pair_ref[base + slot]
            lead = x * jnp.where(spot < first_len, 1.0, 0.0).astype(BF16)
            tail = x - lead
            lead_even = lead * even
            tail_even = tail * even
            parts_of += [lead_even, lead - lead_even, tail_even, tail - tail_even]
            signs.append(jnp.where(first_len % 2 == 0, 1.0, -1.0).astype(F32))
        product = jnp.dot(jnp.concatenate(parts_of, axis=0), table[pair], preferred_element_type=F32)
        end = l_ref[top, pair : pair + 1, :].astype(F32)
        for side in range(2):
            at = 4 * side * rows
            lead_even, lead_odd, tail_even, tail_odd = (
                product[at + i * rows : at + (i + 1) * rows] for i in range(4)
            )
            tail_even = tail_even + last[side] * end
            found = (
                (lead_even + lead_odd, lead_even - lead_odd),
                (tail_even + tail_odd, (tail_even - tail_odd) * signs[side]),
            )
            for which, (north, south) in enumerate(found):
                if side == 0:
                    both = jnp.where(low, north, pltpu.roll(south, LANES // 2, 1))
                else:
                    both = jnp.where(low, pltpu.roll(north, LANES // 2, 1), south)
                wave = 2 * (2 * pair + side) + which
                sums[wave * rows : (wave + 1) * rows, :] = both

    waves = 2 * slots
    share = LANES // parts
    per = LANES // share
    group = iota((waves, LANES), 1) // share
    for step in range(parts):
        index = jnp.broadcast_to(lanes_ref[step : step + 1, :], (waves, LANES))
        for part in range(2):
            for block in range(times // per):
                built = None
                for place in range(per):
                    at = block * per + place
                    step_of, member = at // members, at % members
                    row = (member * steps + step_of) * 2 + part
                    source = sums[pl.ds(row, waves, stride=rows), :]
                    moved = jnp.take_along_axis(source, index, axis=1, mode="promise_in_bounds")
                    built = moved if place == 0 else jnp.where(group == place, moved, built)
                outs[step][part, :, block * LANES : (block + 1) * LANES] = built


def legendre_sums(spectra, turned, pair_of_slot, here, owner, first_unit, units, parts):
    members, steps, _, _, length = spectra.shape
    slots = 2 * PAIRS_UNIT
    waves = 2 * slots
    width = members * steps * LANES // parts
    out = jax.ShapeDtypeStruct((2, units * waves, width), F32)
    return pl.pallas_call(
        functools.partial(legendre_kernel, first_unit, parts),
        grid_spec=pltpu.PrefetchScalarGridSpec(
            num_scalar_prefetch=2,
            grid=(units,),
            in_specs=[
                pl.BlockSpec((1, LANES), lambda u, *_: (0, 0)),
                pl.BlockSpec(
                    (members, steps, slots, 2, length), lambda u, *_: (0, 0, first_unit + u, 0, 0)
                ),
                pl.BlockSpec((length, PAIRS_UNIT, LANES), lambda u, *_: (0, first_unit + u, 0)),
            ],
            out_specs=[pl.BlockSpec((2, waves, width), lambda u, *_: (0, u, 0))] * parts,
            scratch_shapes=[
                pltpu.VMEM((parts, LANES), jnp.int32),
                pltpu.VMEM((PAIRS_UNIT, length - 1, LANES), BF16),
                pltpu.VMEM((waves * 2 * members * steps, LANES), F32),
            ],
        ),
        out_shape=[out] * parts,
        compiler_params=pltpu.CompilerParams(vmem_limit_bytes=VMEM),
        name="legendre",
    )(pair_of_slot, here, owner, spectra, turned)


def split(x):
    high = x.astype(BF16)
    return high, (x - high.astype(F32)).astype(BF16)


def synthesis_kernel(counts, fresh, closing, shape, *refs):
    lon, members, regions, wide = shape
    refs = list(refs)
    if closing:
        starts_ref, here_ref = refs.pop(0), refs.pop(0)
    base_ref, coef_ref = refs.pop(0), refs.pop(0)
    pieces = [refs.pop(0) for _ in counts]
    if not fresh:
        cos_in, sin_in = refs.pop(0), refs.pop(0)
    if closing:
        outs = [refs.pop(0) for _ in range(wide)]
    else:
        cos_out, sin_out = refs.pop(0), refs.pop(0)
    w_cos_h, w_cos_l, w_sin_h, w_sin_l, t_cos_h, t_cos_l, t_sin_h, t_sin_l = refs[:8]
    step = pl.program_id(0)
    block = t_cos_h.shape[0]
    width = pieces[0].shape[2]

    @pl.when(step == 0)
    def _():
        at = 0
        for piece, count in zip(pieces, counts):
            span = slice(at, at + count)
            coef = coef_ref[span, :]
            c, s, rate = coef[:, 0:1], coef[:, 1:2], coef[:, 2:3]
            real, imag = piece[0], piece[1]
            p0 = real * c - imag * s
            p1 = real * s + imag * c
            for index, value in enumerate((p0, rate * p1)):
                cols = slice(index * width, (index + 1) * width)
                w_cos_h[span, cols], w_cos_l[span, cols] = split(value)
            for index, value in enumerate((p1, rate * p0)):
                cols = slice(index * width, (index + 1) * width)
                w_sin_h[span, cols], w_sin_l[span, cols] = split(value)
            at += count

    coarse = lon // 2 // NB

    def fill(a, carry):
        row = step * (block // NB) + a
        ca = base_ref[pl.ds(row, 1), :]
        sa = base_ref[pl.ds(coarse + row, 1), :]
        cb = base_ref[2 * coarse : 2 * coarse + NB, :]
        sb = base_ref[2 * coarse + NB : 2 * coarse + 2 * NB, :]
        at = pl.ds(pl.multiple_of(a * NB, NB), NB)
        t_cos_h[at, :], t_cos_l[at, :] = split(ca * cb - sa * sb)
        t_sin_h[at, :], t_sin_l[at, :] = split(sa * cb + ca * sb)
        return carry

    lax.fori_loop(0, block // NB, fill, 0)

    def product(table_h, table_l, weight_h, weight_l):
        dot = functools.partial(jnp.dot, preferred_element_type=F32)
        return (
            dot(table_h[...], weight_h[...])
            + dot(table_l[...], weight_h[...])
            + dot(table_h[...], weight_l[...])
        )

    even = product(t_cos_h, t_cos_l, w_cos_h, w_cos_l)
    odd = product(t_sin_h, t_sin_l, w_sin_h, w_sin_l)
    if not fresh:
        even = even + cos_in[...]
        odd = odd + sin_in[...]
    if not closing:
        cos_out[...] = even
        sin_out[...] = odd
        return

    value_ref, slope_ref, found_v, found_s = refs[8:]
    half = lon // 2

    def narrowed(x):
        return functools.reduce(
            jnp.maximum, [x[:, i : i + LANES] for i in range(0, width, LANES)]
        )

    a, d = even[:, :width], even[:, width:]
    b, c = odd[:, :width], odd[:, width:]
    below = pl.ds(pl.multiple_of(step * block, block), block)
    above = pl.ds(pl.multiple_of(half + step * block, block), block)
    value_ref[below, :] = narrowed(a + b)
    value_ref[above, :] = narrowed(a - b)
    slope_ref[below, :] = narrowed(jnp.abs(c - d))
    slope_ref[above, :] = narrowed(jnp.abs(c + d))

    @pl.when(step == pl.num_programs(0) - 1)
    def _():
        window = (WIDEST_REGION + 15) // 8 * 8
        rows = iota((window, LANES), 0)

        def best(low, high):
            at = pl.multiple_of(jnp.minimum(low // 8 * 8, lon - window), 8)
            inside = (rows >= low - at) & (rows < high - at)
            v = jnp.where(inside, value_ref[pl.ds(at, window), :], -3e38)
            s = jnp.where(inside, slope_ref[pl.ds(at, window), :], -3e38)
            return jnp.max(v, axis=0, keepdims=True), jnp.max(s, axis=0, keepdims=True)

        def one(region, carry):
            begin, end = starts_ref[region], starts_ref[region + 1]
            upper = end > half
            low = jnp.where(upper, jnp.maximum(begin, half), half - end)
            high = jnp.where(upper, end, half - begin)
            v, s = best(low, high)
            found_v[pl.ds(region, 1), :] = v
            found_s[pl.ds(region, 1), :] = s
            return carry

        lax.fori_loop(0, regions, one, 0, unroll=8)
        centre = starts_ref[regions + 1]
        v, s = best(0, half - starts_ref[centre])
        at = pl.ds(centre, 1)
        found_v[at, :] = jnp.maximum(found_v[at, :], v)
        found_s[at, :] = jnp.maximum(found_s[at, :], s)
        values, slopes = found_v[...], found_s[...]
        span = LANES
        while span > LANES // 2:
            span //= 2
            values = jnp.maximum(values, pltpu.roll(values, span, 1))
            slopes = jnp.maximum(slopes, pltpu.roll(slopes, span, 1))
        found_v[...] = jnp.where(iota(values.shape, 1) < LANES // 2, values, slopes)
        for offset in range(wide):
            owner = lax.rem(here_ref[0] + offset, wide)
            start = pl.multiple_of(owner * REG_DEV, REG_DEV)
            outs[offset][...] = found_v[pl.ds(start, REG_DEV), :]


def synthesis(base, coef, pieces, held, closing, lon, members, regions, wide, starts, here):
    block = min(512, lon // 2)
    depth = base.shape[1]
    counts = tuple(piece.shape[1] for piece in pieces)
    width = pieces[0].shape[2]
    fresh = held is None
    prefetch = (starts, here) if closing else ()
    whole = lambda x: pl.BlockSpec(x.shape, lambda i, *_: (0,) * x.ndim)
    strip = pl.BlockSpec((block, 2 * width), lambda i, *_: (i, 0))
    operands = [base, coef, *pieces] + ([] if fresh else list(held))
    in_specs = [whole(x) for x in (base, coef, *pieces)] + ([] if fresh else [strip] * 2)
    scratch = [pltpu.VMEM((depth, 2 * width), BF16)] * 4 + [pltpu.VMEM((block, depth), BF16)] * 4
    if closing:
        out_shape = [jax.ShapeDtypeStruct((REG_DEV, LANES), F32)] * wide
        out_specs = [pl.BlockSpec((REG_DEV, LANES), lambda i, *_: (0, 0))] * wide
        scratch += [pltpu.VMEM((lon, LANES), F32)] * 2 + [pltpu.VMEM((regions, LANES), F32)] * 2
    else:
        out_shape = [jax.ShapeDtypeStruct((lon // 2, 2 * width), F32)] * 2
        out_specs = [strip] * 2
    return pl.pallas_call(
        functools.partial(
            synthesis_kernel, counts, fresh, closing, (lon, members, regions, wide)
        ),
        grid_spec=pltpu.PrefetchScalarGridSpec(
            num_scalar_prefetch=len(prefetch),
            grid=(lon // 2 // block,),
            in_specs=in_specs,
            out_specs=out_specs,
            scratch_shapes=scratch,
        ),
        out_shape=out_shape,
        compiler_params=pltpu.CompilerParams(vmem_limit_bytes=VMEM),
        name="synthesis",
    )(*prefetch, *operands)


def shift(x, axis, count, step):
    return lax.ppermute(x, axis, [(i, (i + step) % count) for i in range(count)])


def turns(numbers, full):
    angle = (numbers % full).astype(F32) * (2.0 * math.pi / full)
    return jnp.cos(angle), jnp.sin(angle)


def kernels(spectra, legendre, pair_of_slot, lat_owner, region_of_lon):
    members, steps, slot_count, _, length = spectra.shape
    top = length - 1
    lon = region_of_lon.shape[0]
    parts = lax.axis_size("narrow")
    wide = lax.axis_size("wide")
    regions = REG_DEV * wide
    here = lax.axis_index("narrow")
    here_wide = lax.axis_index("wide")
    here_ref = here.reshape(1)
    owner = lat_owner.reshape(1, -1)
    turned = jnp.transpose(legendre, (1, 0, 2))

    chunks, first = [], 0
    for units in CHUNKS:
        sums = legendre_sums(
            spectra, turned, pair_of_slot, here_ref, owner, first, units, parts
        )
        chunks.append([sums[0]] + [shift(sums[i], "narrow", parts, i) for i in range(1, parts)])
        final, first = sums[0], first + units
    pair_of_slot, region_of_lon, final = lax.optimization_barrier(
        (pair_of_slot, region_of_lon, final)
    )
    chunks[-1][0] = final

    waves_of = jnp.stack([pair_of_slot, top - 1 - pair_of_slot], axis=1).reshape(parts, -1)
    source = lax.rem(here - jnp.arange(parts, dtype=jnp.int32) + parts, parts)
    waves_of = waves_of[source]
    edges = jnp.arange(regions + 1, dtype=jnp.int32)
    starts = jnp.sum((region_of_lon[None, :] < edges[:, None]).astype(jnp.int32), axis=1)
    starts = jnp.concatenate([starts, region_of_lon[lon // 2 - 1 : lon // 2]])

    per_unit = 4 * PAIRS_UNIT
    bounds = [0]
    for units in CHUNKS:
        bounds.append(bounds[-1] + units * per_unit)
    order = []
    for stage in STAGES:
        for chunk in stage:
            order.append(waves_of[:, bounds[chunk] : bounds[chunk + 1]].reshape(-1))
    waves = jnp.concatenate(order)
    full = 8 * top
    coarse = 2 * NB * jnp.arange(lon // 2 // NB, dtype=jnp.int32)
    fine = 2 * jnp.arange(NB, dtype=jnp.int32) + 1
    ca, sa = turns(coarse[:, None] * waves[None, :], full)
    cb, sb = turns(fine[:, None] * waves[None, :], full)
    base = jnp.concatenate([ca, sa, cb, sb], axis=0)
    c, s = turns((lon - 1) * waves, full)
    scale = top ** (-0.5)
    coef = jnp.stack([c * scale, s * scale, waves.astype(F32) / top] + [c] * 5, axis=1)

    held, at = None, 0
    for number, stage in enumerate(STAGES):
        pieces = [piece for chunk in stage for piece in chunks[chunk]]
        depth = sum(piece.shape[1] for piece in pieces)
        held = synthesis(
            base[:, at : at + depth],
            coef[at : at + depth],
            pieces,
            held,
            number == len(STAGES) - 1,
            lon,
            members,
            regions,
            wide,
            starts,
            here_wide.reshape(1),
        )
        at += depth

    best = held[0]
    for offset in range(1, wide):
        best = jnp.maximum(best, shift(held[offset], "wide", wide, offset))
    best = best.reshape(REG_DEV, 2, members, LANES // 2 // members)
    peak = jnp.transpose(best[:, 0], (1, 2, 0))
    peak_slope = jnp.transpose(best[:, 1], (1, 2, 0))
    return peak, peak_slope


def per_device(spectra, legendre, pair_of_slot, lat_owner, region_of_lon):
    members, steps, _, _, length = spectra.shape
    pairs, _, lanes = legendre.shape
    share = lat_owner.shape[0] // lax.axis_size("narrow")
    fits = (
        pairs == PAIRS_UNIT * sum(CHUNKS)
        and lanes == LANES
        and lat_owner.shape[0] == LANES
        and 2 * members * share == LANES
        and members * steps * share % LANES == 0
        and (length - 1) % LANES == 0
        and region_of_lon.shape[0] % 1024 == 0
    )
    run = kernels if fits else plain
    return run(spectra, legendre, pair_of_slot, lat_owner, region_of_lon)


def solution(mesh):
    in_specs = (
        P(None, ("groups", "wide"), "narrow", None, None),
        P("narrow", None, None),
        P(),
        P(),
        P(),
    )
    out_specs = (P("groups", "narrow", "wide"), P("groups", "narrow", "wide"))
    return jax.shard_map(
        per_device, mesh=mesh, in_specs=in_specs, out_specs=out_specs, check_vma=False
    )
```

```python
import functools
import math

import jax
import jax.numpy as jnp
from jax import lax
from jax.experimental import pallas as pl
from jax.experimental.pallas import tpu as pltpu
from jax.sharding import PartitionSpec as P

REG_DEV = 16
WIDEST_REGION = 48
LANES = 128
PAIRS_UNIT = 8
NB = 32
CUTS = 5
LEGENDRE_VMEM = 107 * 2**19
SYNTHESIS_VMEM = 28 * 2**20
TURN = 128
CHUNKS = (2, 2, 2, 2, 2)
GROUPS = ((0, 1), (2, 3), (4,))
F32 = jnp.float32
BF16 = jnp.bfloat16


def synthesize(operand, waves, start, width, top):
    columns = start + jnp.arange(width, dtype=jnp.int32)
    phase = waves[:, None] * columns[None, :] % (4 * top)
    angle = phase.astype(F32) * (2.0 * math.pi / (4 * top))
    cosine = jnp.cos(angle)
    sine = jnp.sin(angle)
    rate = (waves.astype(F32) / top)[:, None]
    upper = jnp.concatenate([cosine, -rate * sine], axis=1)
    lower = jnp.concatenate([-sine, -rate * cosine], axis=1)
    table = jnp.concatenate([upper, lower], axis=0) * top ** (-0.5)
    return jnp.dot(operand, table, precision=lax.Precision.HIGHEST)


def synthesize_all(operand, waves, lon, top):
    width = min(512, lon)
    starts = jnp.arange(lon // width, dtype=jnp.int32) * width
    blocks = lax.map(lambda begin: synthesize(operand, waves, begin, width, top), starts)
    blocks = blocks.reshape(blocks.shape[0], blocks.shape[1], 2, width)
    value = jnp.transpose(blocks[:, :, 0], (1, 0, 2)).reshape(operand.shape[0], lon)
    slope = jnp.transpose(blocks[:, :, 1], (1, 0, 2)).reshape(operand.shape[0], lon)
    return value, slope


def region_peak(values, region_of_lon, wanted):
    hits = region_of_lon[:, None] == wanted[None, :]
    masked = jnp.where(hits[None, None], values[..., None], -1e30)
    return masked.max(axis=2)


def plain(spectra, legendre, pair_of_slot, lat_owner, region_of_lon):
    members, steps_here, slot_count, _, length = spectra.shape
    top = length - 1
    lon = region_of_lon.shape[0]
    half_count = legendre.shape[0]
    lat_half = legendre.shape[2] // 2
    here = lax.axis_index("narrow")
    paired = lax.dynamic_slice_in_dim(pair_of_slot, here * slot_count, slot_count)
    position = jnp.arange(length, dtype=jnp.int32)[None, :]
    first_len = (top - paired)[:, None]
    leading = position < first_len
    offset = jnp.where(leading, position, position - first_len)
    even_term = offset % 2 == 0
    masks = jnp.stack(
        [leading & even_term, leading & ~even_term, ~leading & even_term, ~leading & ~even_term],
        axis=1,
    ).astype(BF16)
    ordered = jnp.transpose(spectra, (2, 0, 1, 3, 4))
    masked = masks[:, :, None, None, None, :] * ordered[:, None]
    masked = masked.reshape(half_count, 2, -1, length)
    table = legendre.reshape(half_count, length, 2, lat_half)
    sums = jnp.einsum("abrl,albj->abrj", masked, table, preferred_element_type=F32)
    sums = sums.reshape(slot_count, 4, members, steps_here, 2, lat_half)
    north_lead = sums[:, 0] + sums[:, 1]
    south_lead = sums[:, 0] - sums[:, 1]
    north_tail = sums[:, 2] + sums[:, 3]
    south_tail = sums[:, 2] - sums[:, 3]
    lead = jnp.concatenate([north_lead, jnp.flip(south_lead, axis=-1)], axis=-1)
    tail = jnp.concatenate([north_tail, jnp.flip(south_tail, axis=-1)], axis=-1)
    waved = jnp.stack([lead, tail], axis=1).reshape(2 * slot_count, members, steps_here, 2, -1)
    order = jnp.argsort(lat_owner, stable=True)
    waved = jnp.take(waved, order, axis=4)
    arrived = lax.all_to_all(waved, "narrow", split_axis=4, concat_axis=0, tiled=True)
    waves = jnp.stack([pair_of_slot, top - 1 - pair_of_slot], axis=1).reshape(-1)
    lat_here = arrived.shape[4]
    operand = jnp.transpose(arrived, (1, 2, 4, 3, 0)).reshape(members * steps_here * lat_here, -1)
    value, slope = synthesize_all(operand, waves, lon, top)
    value = value.reshape(members, steps_here, lat_here, lon).max(axis=1)
    slope = jnp.abs(slope).reshape(members, steps_here, lat_here, lon).max(axis=1)
    wide_count = lax.axis_size("wide")
    mine_start = lax.axis_index("wide") * REG_DEV
    wanted = jnp.arange(REG_DEV * wide_count, dtype=jnp.int32)
    peaks = region_peak(value, region_of_lon, wanted)
    slopes = region_peak(slope, region_of_lon, wanted)
    peaks, slopes = lax.pmax((peaks, slopes), "wide")
    peak = lax.dynamic_slice_in_dim(peaks, mine_start, REG_DEV, 2)
    peak_slope = lax.dynamic_slice_in_dim(slopes, mine_start, REG_DEV, 2)
    return peak, peak_slope


def iota(shape, axis):
    return lax.broadcasted_iota(jnp.int32, shape, axis)


def latitude_lanes(owner, here, parts):
    square = (LANES, LANES)
    row = jnp.broadcast_to(owner.astype(F32), square)
    column = row.T
    first, second = iota(square, 0), iota(square, 1)
    ahead = (column < row) | ((column == row) & (first < second))
    place = jnp.sum(jnp.where(ahead, 1.0, 0.0), axis=0, keepdims=True)
    place = jnp.broadcast_to(place, square).T
    half = LANES // 2
    lane_of = jnp.where(first < half, first, half + LANES - 1 - first).astype(F32)
    share = LANES // parts
    rows = []
    for step in range(parts):
        owner_index = lax.bitwise_xor(here, jnp.int32(step))
        target = (owner_index * share + second % share).astype(F32)
        rows.append(jnp.sum(jnp.where(place == target, lane_of, 0.0), axis=0, keepdims=True))
    return jnp.concatenate(rows, axis=0).astype(jnp.int32)


def legendre_kernel(first_unit, units, parts, known, pair_ref, here_ref, owner_ref, s_hbm, l_hbm, *refs):
    if known:
        lanes_ref, outs, refs = owner_ref, refs[:parts], refs[parts:]
    else:
        lanes_ref, outs, refs = refs[parts], refs[:parts], refs[parts + 1 :]
    s_buf, l_buf, table, total, sums, ends, s_sem, l_sem = refs
    _, members, steps, slots, _, length = s_buf.shape
    top = length - 1
    times = members * steps
    rows = 2 * times
    pairs = slots // 2
    unit = pl.program_id(0)
    here = here_ref[0]
    cuts = l_sem.shape[1]
    depth = top // cuts

    def copies(which):
        side = lax.rem(which, 2)
        at = pl.multiple_of((first_unit + which) * slots, slots)
        found = [
            pltpu.make_async_copy(
                s_hbm.at[:, :, pl.ds(at, slots)], s_buf.at[side], s_sem.at[side]
            )
        ]
        at = pl.multiple_of((first_unit + which) * pairs, pairs)
        for cut in range(cuts):
            span = pl.ds(cut * depth, depth if cut < cuts - 1 else length - cut * depth)
            found.append(
                pltpu.make_async_copy(
                    l_hbm.at[span, pl.ds(at, pairs)], l_buf.at[side, span], l_sem.at[side, cut]
                )
            )
        return found

    @pl.when(unit == 0)
    def _():
        for copy in copies(jnp.int32(0)):
            copy.start()
        if not known:
            lanes_ref[...] = latitude_lanes(owner_ref[...], here, parts)

    @pl.when(unit + 1 < units)
    def _():
        for copy in copies(unit + 1):
            copy.start()

    side = lax.rem(unit, 2)
    arriving = copies(unit)
    arriving[0].wait()

    spot = iota((rows, top), 1)
    even = jnp.where(spot % 2 == 0, 1.0, 0.0).astype(BF16)
    base = here * (pair_ref.shape[0] // parts) + (first_unit + unit) * slots
    for cut in range(cuts):
        arriving[1 + cut].wait()
        for at in range(cut * depth, (cut + 1) * depth, TURN):
            table[:, at : at + TURN, :] = jnp.swapaxes(l_buf[side, at : at + TURN], 0, 1)

    for pair in range(pairs):
        masked = []
        for slot in (2 * pair, 2 * pair + 1):
            x = s_buf[side, :, :, slot].reshape(rows, length)[:, :top]
            first_len = top - pair_ref[base + slot]
            lead = x * jnp.where(spot < first_len, 1.0, 0.0).astype(BF16)
            tail = x - lead
            lead_even = lead * even
            tail_even = tail * even
            masked += [lead_even, lead - lead_even, tail_even, tail - tail_even]
        total[pair] = jnp.dot(
            jnp.concatenate(masked, axis=0), table[pair], preferred_element_type=F32
        )

    low = iota((rows, LANES), 1) < LANES // 2

    ends[...] = l_buf[side, top].astype(F32)

    def combine(pair, carry):
        end = ends[pl.ds(pair, 1), :]
        for odd_slot in range(2):
            slot = 2 * pair + odd_slot
            sign = jnp.where((top - pair_ref[base + slot]) % 2 == 0, 1.0, -1.0).astype(F32)
            last = s_buf[side, :, :, slot, :, top:].reshape(rows, 1).astype(F32)
            at = 4 * odd_slot * rows
            lead_even, lead_odd, tail_even, tail_odd = (
                total[pair, at + i * rows : at + (i + 1) * rows, :] for i in range(4)
            )
            tail_even = tail_even + last * end
            found = (
                (lead_even + lead_odd, lead_even - lead_odd),
                (tail_even + tail_odd, (tail_even - tail_odd) * sign),
            )
            for which, (north, south) in enumerate(found):
                if odd_slot:
                    both = jnp.where(low, pltpu.roll(north, LANES // 2, 1), south)
                else:
                    both = jnp.where(low, north, pltpu.roll(south, LANES // 2, 1))
                at = pl.multiple_of((2 * slot + which) * rows, rows)
                sums[pl.ds(at, rows), :] = both
        return carry

    [combine(i, 0) for i in range(pairs)]

    waves = 2 * slots
    share = LANES // parts
    per = LANES // share
    group = iota((waves, LANES), 1) // share
    mine = pl.ds(pl.multiple_of(unit * waves, waves), waves)
    for step in range(parts):
        index = jnp.broadcast_to(lanes_ref[step : step + 1, :], (waves, LANES))
        for part in range(2):
            for block in range(times // per):
                built = None
                for place in range(per):
                    at = block * per + place
                    step_of, member = at // members, at % members
                    row = (member * steps + step_of) * 2 + part
                    source = sums[pl.ds(row, waves, stride=rows), :]
                    moved = jnp.take_along_axis(source, index, axis=1, mode="promise_in_bounds")
                    built = moved if place == 0 else jnp.where(group == place, moved, built)
                outs[step][part, mine, block * LANES : (block + 1) * LANES] = built


def legendre_sums(spectra, turned, pair_of_slot, here, owner, first_unit, units, parts):
    members, steps, _, _, length = spectra.shape
    slots = 2 * PAIRS_UNIT
    waves = 2 * slots
    times = members * steps
    width = times * LANES // parts
    known = first_unit > 0
    out = [jax.ShapeDtypeStruct((2, units * waves, width), F32)] * parts
    if not known:
        out = out + [jax.ShapeDtypeStruct((parts, LANES), jnp.int32)]
    here_spec = pl.BlockSpec(memory_space=pltpu.VMEM)
    away = pl.BlockSpec(memory_space=pltpu.HBM)
    return pl.pallas_call(
        functools.partial(legendre_kernel, first_unit, units, parts, known),
        grid_spec=pltpu.PrefetchScalarGridSpec(
            num_scalar_prefetch=2,
            grid=(units,),
            in_specs=[here_spec, away, away],
            out_specs=[here_spec] * len(out),
            scratch_shapes=[
                pltpu.VMEM((2, members, steps, slots, 2, length), BF16),
                pltpu.VMEM((2, length, PAIRS_UNIT, LANES), BF16),
                pltpu.VMEM((PAIRS_UNIT, length - 1, LANES), BF16),
                pltpu.VMEM((PAIRS_UNIT, 16 * times, LANES), F32),
                pltpu.VMEM((waves * 2 * times, LANES), F32),
                pltpu.VMEM((PAIRS_UNIT, LANES), F32),
                pltpu.SemaphoreType.DMA((2,)),
                pltpu.SemaphoreType.DMA((2, CUTS)),
            ],
        ),
        out_shape=out,
        compiler_params=pltpu.CompilerParams(vmem_limit_bytes=LEGENDRE_VMEM),
        cost_estimate=pl.CostEstimate(
            flops=units * PAIRS_UNIT * 2 * LANES * LANES * length,
            bytes_accessed=units * PAIRS_UNIT * (LANES + 2 * 2 * times) * length * 2,
            transcendentals=0,
        ),
        name="legendre",
    )(pair_of_slot, here, owner, spectra, turned)


def split(x):
    high = x.astype(BF16)
    return high, (x - high.astype(F32)).astype(BF16)


def turns(numbers, full):
    quarter = full // 4
    turned = (numbers + quarter // 2) // quarter
    x = (numbers - turned * quarter).astype(F32) * (2.0 * math.pi / full)
    y = x * x
    sine = x * (1.0 + y * (-1 / 6 + y * (1 / 120 + y * (-1 / 5040 + y * (1 / 362880)))))
    cosine = 1.0 + y * (-1 / 2 + y * (1 / 24 + y * (-1 / 720 + y * (1 / 40320 - y * (1 / 3628800)))))
    odd = turned % 2 == 1
    c, s = jnp.where(odd, sine, cosine), jnp.where(odd, cosine, sine)
    c = jnp.where((turned == 1) | (turned == 2), -c, c)
    s = jnp.where((turned == 2) | (turned == 3), -s, s)
    return c, s


def synthesis_kernel(counts, fresh, closing, shape, *refs):
    lon, top, regions, wide = shape
    refs = list(refs)
    if closing:
        starts_ref, here_ref = refs.pop(0), refs.pop(0)
    waves_ref = refs.pop(0)
    pieces = [refs.pop(0) for _ in counts]
    if not fresh:
        cos_in, sin_in = refs.pop(0), refs.pop(0)
    if closing:
        outs = [refs.pop(0) for _ in range(wide)]
    else:
        cos_out, sin_out = refs.pop(0), refs.pop(0)
    base_ref, w_cos_h, w_cos_l, w_sin_h, w_sin_l, t_cos_h, t_cos_l, t_sin_h, t_sin_l = refs[:9]
    step = pl.program_id(0)
    block, depth = t_cos_h.shape
    width = pieces[0].shape[2]
    coarse = lon // 2 // NB
    full = 8 * top

    @pl.when(step == 0)
    def _():
        waves = waves_ref[...]
        at = 0
        for factor, shift_by, count in ((2 * NB, 0, coarse), (2, 1, NB)):
            number = factor * iota((count, depth), 0) + shift_by
            c, s = turns(number * waves % full, full)
            base_ref[at : at + count, :] = c
            base_ref[at + count : at + 2 * count, :] = s
            at += 2 * count
        c, s = turns((lon - 1) * waves % full, full)
        rate = waves.astype(F32) * (1.0 / top)
        scale = top ** (-0.5)
        kind = iota((8, depth), 0)
        turn = jnp.where(kind == 0, c * scale, jnp.where(kind == 1, s * scale, rate))
        at = 0
        for piece, count in zip(pieces, counts):
            span = slice(at, at + count)
            coef = turn[:, span].T
            c, s, rate = coef[:, 0:1], coef[:, 1:2], coef[:, 2:3]
            real, imag = piece[0], piece[1]
            p0 = real * c - imag * s
            p1 = real * s + imag * c
            for index, value in enumerate((p0, rate * p1)):
                cols = slice(index * width, (index + 1) * width)
                w_cos_h[span, cols], w_cos_l[span, cols] = split(value)
            for index, value in enumerate((p1, rate * p0)):
                cols = slice(index * width, (index + 1) * width)
                w_sin_h[span, cols], w_sin_l[span, cols] = split(value)
            at += count

    def fill(a, carry):
        row = step * (block // NB) + a
        ca = base_ref[pl.ds(row, 1), :]
        sa = base_ref[pl.ds(coarse + row, 1), :]
        cb = base_ref[2 * coarse : 2 * coarse + NB, :]
        sb = base_ref[2 * coarse + NB : 2 * coarse + 2 * NB, :]
        at = pl.ds(pl.multiple_of(a * NB, NB), NB)
        t_cos_h[at, :], t_cos_l[at, :] = split(ca * cb - sa * sb)
        t_sin_h[at, :], t_sin_l[at, :] = split(sa * cb + ca * sb)
        return carry

    lax.fori_loop(0, block // NB, fill, 0)

    def product(table_h, table_l, weight_h, weight_l):
        dot = functools.partial(jnp.dot, preferred_element_type=F32)
        return (
            dot(table_h[...], weight_h[...])
            + dot(table_l[...], weight_h[...])
            + dot(table_h[...], weight_l[...])
        )

    even = product(t_cos_h, t_cos_l, w_cos_h, w_cos_l)
    odd = product(t_sin_h, t_sin_l, w_sin_h, w_sin_l)
    here_rows = pl.ds(pl.multiple_of(step * block, block), block)
    if not fresh:
        even = even + cos_in[here_rows, :]
        odd = odd + sin_in[here_rows, :]
    if not closing:
        cos_out[here_rows, :] = even
        sin_out[here_rows, :] = odd
        return

    value_ref, slope_ref, found_v, found_s = refs[9:]
    half = lon // 2

    def narrowed(x):
        return functools.reduce(
            jnp.maximum, [x[:, i : i + LANES] for i in range(0, width, LANES)]
        )

    a, d = even[:, :width], even[:, width:]
    b, c = odd[:, :width], odd[:, width:]
    below = pl.ds(pl.multiple_of(step * block, block), block)
    above = pl.ds(pl.multiple_of(half + step * block, block), block)
    value_ref[below, :] = narrowed(a + b)
    value_ref[above, :] = narrowed(a - b)
    slope_ref[below, :] = narrowed(jnp.abs(c - d))
    slope_ref[above, :] = narrowed(jnp.abs(c + d))

    @pl.when(step == pl.num_programs(0) - 1)
    def _():
        window = (WIDEST_REGION + 15) // 8 * 8
        rows = iota((window, LANES), 0)

        def best(low, high):
            at = pl.multiple_of(jnp.minimum(low // 8 * 8, lon - window), 8)
            inside = (rows >= low - at) & (rows < high - at)
            v = jnp.where(inside, value_ref[pl.ds(at, window), :], -3e38)
            s = jnp.where(inside, slope_ref[pl.ds(at, window), :], -3e38)
            return jnp.max(v, axis=0, keepdims=True), jnp.max(s, axis=0, keepdims=True)

        def one(region, carry):
            begin, end = starts_ref[region], starts_ref[region + 1]
            upper = end > half
            low = jnp.where(upper, jnp.maximum(begin, half), half - end)
            high = jnp.where(upper, end, half - begin)
            v, s = best(low, high)
            found_v[pl.ds(region, 1), :] = v
            found_s[pl.ds(region, 1), :] = s
            return carry

        lax.fori_loop(0, regions, one, 0, unroll=8)
        centre = starts_ref[regions + 1]
        v, s = best(0, half - starts_ref[centre])
        at = pl.ds(centre, 1)
        found_v[at, :] = jnp.maximum(found_v[at, :], v)
        found_s[at, :] = jnp.maximum(found_s[at, :], s)
        values, slopes = found_v[...], found_s[...]
        span = LANES
        while span > LANES // 2:
            span //= 2
            values = jnp.maximum(values, pltpu.roll(values, span, 1))
            slopes = jnp.maximum(slopes, pltpu.roll(slopes, span, 1))
        found_v[...] = jnp.where(iota(values.shape, 1) < LANES // 2, values, slopes)
        for offset in range(wide):
            owner = lax.rem(here_ref[0] + offset, wide)
            start = pl.multiple_of(owner * REG_DEV, REG_DEV)
            outs[offset][...] = found_v[pl.ds(start, REG_DEV), :]


def synthesis(waves, pieces, held, closing, lon, top, regions, wide, starts, here):
    block = min(512, lon // 2)
    depth = waves.shape[1]
    counts = tuple(piece.shape[1] for piece in pieces)
    width = pieces[0].shape[2]
    fresh = held is None
    prefetch = (starts, here) if closing else ()
    operands = [waves, *pieces] + ([] if fresh else list(held))
    in_specs = [pl.BlockSpec(memory_space=pltpu.VMEM)] * len(operands)
    scratch = [pltpu.VMEM((2 * (lon // 2 // NB + NB), depth), F32)]
    scratch += [pltpu.VMEM((depth, 2 * width), BF16)] * 4 + [pltpu.VMEM((block, depth), BF16)] * 4
    if closing:
        out_shape = [jax.ShapeDtypeStruct((REG_DEV, LANES), F32)] * wide
        scratch += [pltpu.VMEM((lon, LANES), F32)] * 2 + [pltpu.VMEM((regions, LANES), F32)] * 2
    else:
        out_shape = [jax.ShapeDtypeStruct((lon // 2, 2 * width), F32)] * 2
    out_specs = [pl.BlockSpec(memory_space=pltpu.VMEM)] * len(out_shape)
    return pl.pallas_call(
        functools.partial(
            synthesis_kernel, counts, fresh, closing, (lon, top, regions, wide)
        ),
        grid_spec=pltpu.PrefetchScalarGridSpec(
            num_scalar_prefetch=len(prefetch),
            grid=(lon // 2 // block,),
            in_specs=in_specs,
            out_specs=out_specs,
            scratch_shapes=scratch,
        ),
        out_shape=out_shape,
        compiler_params=pltpu.CompilerParams(vmem_limit_bytes=SYNTHESIS_VMEM),
        cost_estimate=pl.CostEstimate(
            flops=6 * depth * lon * 2 * width, bytes_accessed=16 * lon * width, transcendentals=0
        ),
        name="synthesis",
    )(*prefetch, *operands)


def shift(x, axis, count, step):
    return lax.ppermute(x, axis, [(i, (i + step) % count) for i in range(count)])


def swap(x, axis, count, step):
    return lax.ppermute(x, axis, [(i, i ^ step) for i in range(count)])


def final_kernel(*refs):
    *found, peak_ref, slope_ref = refs
    best = functools.reduce(jnp.maximum, [x[...] for x in found])
    members, _, share = peak_ref.shape
    for member in range(members):
        peak_ref[member] = best[:, member * share : (member + 1) * share]
        at = LANES // 2 + member * share
        slope_ref[member] = best[:, at : at + share]


def kernels(spectra, legendre, pair_of_slot, lat_owner, region_of_lon):
    members, steps, slot_count, _, length = spectra.shape
    top = length - 1
    lon = region_of_lon.shape[0]
    parts = lax.axis_size("narrow")
    wide = lax.axis_size("wide")
    regions = REG_DEV * wide
    here = lax.axis_index("narrow")
    here_wide = lax.axis_index("wide")
    here_ref = here.reshape(1)
    owner = lat_owner.reshape(1, -1)
    turned = jnp.transpose(legendre, (1, 0, 2))
    tied = lax.optimization_barrier

    kept, beside, near, far, first = [], [], [], [], 0
    for number, units in enumerate(CHUNKS):
        if number >= 1:
            here_ref, kept[-1] = tied((here_ref, kept[-1]))
        if number == 2:
            pair_here, region_of_lon, kept[-1] = tied((pair_of_slot, region_of_lon, kept[-1]))
        if number >= 2:
            here_ref, far[number - 2] = tied((here_ref, far[number - 2]))
        if number >= 3:
            ready = [g for g, group in enumerate(GROUPS) if group[-1] == number - 2]
            for g in ready:
                here_ref, near[g] = tied((here_ref, near[g]))
        sums = legendre_sums(
            spectra, turned, pair_of_slot, here_ref, owner, first, units, parts
        )
        if number == 0:
            owner = sums[parts]
        kept.append(sums[0])
        beside.append(sums[1])
        far.append([swap(sums[i], "narrow", parts, i) for i in range(2, parts)])
        for group in GROUPS:
            if group[-1] == number:
                near.append(swap(jnp.concatenate([beside[i] for i in group], axis=1), "narrow", parts, 1))
        first += units

    waves_of = jnp.stack([pair_here, top - 1 - pair_here], axis=1).reshape(parts, -1)
    waves_of = waves_of[lax.bitwise_xor(here, jnp.arange(parts, dtype=jnp.int32))]
    edges = jnp.arange(regions + 1, dtype=jnp.int32)
    starts = jnp.sum((region_of_lon[None, :] < edges[:, None]).astype(jnp.int32), axis=1)
    starts = jnp.concatenate([starts, region_of_lon[lon // 2 - 1 : lon // 2]])

    per_unit = 4 * PAIRS_UNIT
    bounds = [0]
    for units in CHUNKS:
        bounds.append(bounds[-1] + units * per_unit)

    def piece(array, source, chunks):
        return array, [waves_of[source, bounds[i] : bounds[i + 1]] for i in chunks]

    late = len(CHUNKS) - 1
    own = [piece(kept[i], 0, (i,)) for i in range(late + 1)]
    swapped = [piece(near[g], 1, group) for g, group in enumerate(GROUPS)]
    across = [
        [piece(array, 2 + i, (chunk,)) for i, array in enumerate(far[chunk])]
        for chunk in range(late + 1)
    ]
    stages = (
        own[: late - 1] + swapped[:-2] + sum(across[: late - 1], []),
        own[late - 1 :] + swapped[-2:-1] + across[late - 1],
        swapped[-1:] + across[late],
    )
    held = None
    for number, stage in enumerate(stages):
        waves = jnp.concatenate([w for _, found in stage for w in found])
        held = synthesis(
            waves.reshape(1, -1),
            [array for array, _ in stage],
            held,
            number == len(stages) - 1,
            lon,
            top,
            regions,
            wide,
            starts,
            here_wide.reshape(1),
        )

    found = [held[0]] + [shift(held[i], "wide", wide, i) for i in range(1, wide)]
    out = jax.ShapeDtypeStruct((members, REG_DEV, LANES // 2 // members), F32)
    peak, peak_slope = pl.pallas_call(final_kernel, out_shape=[out] * 2, name="final")(*found)
    return jnp.transpose(peak, (0, 2, 1)), jnp.transpose(peak_slope, (0, 2, 1))


def per_device(spectra, legendre, pair_of_slot, lat_owner, region_of_lon):
    members, steps, _, _, length = spectra.shape
    pairs, _, lanes = legendre.shape
    share = lat_owner.shape[0] // lax.axis_size("narrow")
    parts = lax.axis_size("narrow")
    fits = (
        parts & (parts - 1) == 0
        and pairs == PAIRS_UNIT * sum(CHUNKS)
        and lanes == LANES
        and lat_owner.shape[0] == LANES
        and 2 * members * share == LANES
        and members * steps * share % LANES == 0
        and (length - 1) % LANES == 0
        and region_of_lon.shape[0] % 1024 == 0
    )
    run = kernels if fits else plain
    return run(spectra, legendre, pair_of_slot, lat_owner, region_of_lon)


def solution(mesh):
    in_specs = (
        P(None, ("groups", "wide"), "narrow", None, None),
        P("narrow", None, None),
        P(),
        P(),
        P(),
    )
    out_specs = (P("groups", "narrow", "wide"), P("groups", "narrow", "wide"))
    return jax.shard_map(
        per_device, mesh=mesh, in_specs=in_specs, out_specs=out_specs, check_vma=False
    )
```

```python
import functools
import math

import jax
import jax.numpy as jnp
from jax import lax
from jax.experimental import pallas as pl
from jax.experimental.pallas import tpu as pltpu
from jax.sharding import PartitionSpec as P

REG_DEV = 16
WIDEST_REGION = 48
LANES = 128
PAIRS_UNIT = 8
NB = 32
CUTS = 5
LEGENDRE_VMEM = 107 * 2**19
SYNTHESIS_VMEM = 24 * 2**20
TABLES_VMEM = 12 * 2**20
TURN = 128
CHUNKS = (2, 3, 3, 2)
GROUPS = ((0, 1, 2), (3,))
F32 = jnp.float32
BF16 = jnp.bfloat16


def synthesize(operand, waves, start, width, top):
    columns = start + jnp.arange(width, dtype=jnp.int32)
    phase = waves[:, None] * columns[None, :] % (4 * top)
    angle = phase.astype(F32) * (2.0 * math.pi / (4 * top))
    cosine = jnp.cos(angle)
    sine = jnp.sin(angle)
    rate = (waves.astype(F32) / top)[:, None]
    upper = jnp.concatenate([cosine, -rate * sine], axis=1)
    lower = jnp.concatenate([-sine, -rate * cosine], axis=1)
    table = jnp.concatenate([upper, lower], axis=0) * top ** (-0.5)
    return jnp.dot(operand, table, precision=lax.Precision.HIGHEST)


def synthesize_all(operand, waves, lon, top):
    width = min(512, lon)
    starts = jnp.arange(lon // width, dtype=jnp.int32) * width
    blocks = lax.map(lambda begin: synthesize(operand, waves, begin, width, top), starts)
    blocks = blocks.reshape(blocks.shape[0], blocks.shape[1], 2, width)
    value = jnp.transpose(blocks[:, :, 0], (1, 0, 2)).reshape(operand.shape[0], lon)
    slope = jnp.transpose(blocks[:, :, 1], (1, 0, 2)).reshape(operand.shape[0], lon)
    return value, slope


def region_peak(values, region_of_lon, wanted):
    hits = region_of_lon[:, None] == wanted[None, :]
    masked = jnp.where(hits[None, None], values[..., None], -1e30)
    return masked.max(axis=2)


def plain(spectra, legendre, pair_of_slot, lat_owner, region_of_lon):
    members, steps_here, slot_count, _, length = spectra.shape
    top = length - 1
    lon = region_of_lon.shape[0]
    half_count = legendre.shape[0]
    lat_half = legendre.shape[2] // 2
    here = lax.axis_index("narrow")
    paired = lax.dynamic_slice_in_dim(pair_of_slot, here * slot_count, slot_count)
    position = jnp.arange(length, dtype=jnp.int32)[None, :]
    first_len = (top - paired)[:, None]
    leading = position < first_len
    offset = jnp.where(leading, position, position - first_len)
    even_term = offset % 2 == 0
    masks = jnp.stack(
        [leading & even_term, leading & ~even_term, ~leading & even_term, ~leading & ~even_term],
        axis=1,
    ).astype(BF16)
    ordered = jnp.transpose(spectra, (2, 0, 1, 3, 4))
    masked = masks[:, :, None, None, None, :] * ordered[:, None]
    masked = masked.reshape(half_count, 2, -1, length)
    table = legendre.reshape(half_count, length, 2, lat_half)
    sums = jnp.einsum("abrl,albj->abrj", masked, table, preferred_element_type=F32)
    sums = sums.reshape(slot_count, 4, members, steps_here, 2, lat_half)
    north_lead = sums[:, 0] + sums[:, 1]
    south_lead = sums[:, 0] - sums[:, 1]
    north_tail = sums[:, 2] + sums[:, 3]
    south_tail = sums[:, 2] - sums[:, 3]
    lead = jnp.concatenate([north_lead, jnp.flip(south_lead, axis=-1)], axis=-1)
    tail = jnp.concatenate([north_tail, jnp.flip(south_tail, axis=-1)], axis=-1)
    waved = jnp.stack([lead, tail], axis=1).reshape(2 * slot_count, members, steps_here, 2, -1)
    order = jnp.argsort(lat_owner, stable=True)
    waved = jnp.take(waved, order, axis=4)
    arrived = lax.all_to_all(waved, "narrow", split_axis=4, concat_axis=0, tiled=True)
    waves = jnp.stack([pair_of_slot, top - 1 - pair_of_slot], axis=1).reshape(-1)
    lat_here = arrived.shape[4]
    operand = jnp.transpose(arrived, (1, 2, 4, 3, 0)).reshape(members * steps_here * lat_here, -1)
    value, slope = synthesize_all(operand, waves, lon, top)
    value = value.reshape(members, steps_here, lat_here, lon).max(axis=1)
    slope = jnp.abs(slope).reshape(members, steps_here, lat_here, lon).max(axis=1)
    wide_count = lax.axis_size("wide")
    mine_start = lax.axis_index("wide") * REG_DEV
    wanted = jnp.arange(REG_DEV * wide_count, dtype=jnp.int32)
    peaks = region_peak(value, region_of_lon, wanted)
    slopes = region_peak(slope, region_of_lon, wanted)
    peaks, slopes = lax.pmax((peaks, slopes), "wide")
    peak = lax.dynamic_slice_in_dim(peaks, mine_start, REG_DEV, 2)
    peak_slope = lax.dynamic_slice_in_dim(slopes, mine_start, REG_DEV, 2)
    return peak, peak_slope


def iota(shape, axis):
    return lax.broadcasted_iota(jnp.int32, shape, axis)


def latitude_lanes(owner, here, parts):
    square = (LANES, LANES)
    row = jnp.broadcast_to(owner.astype(F32), square)
    column = row.T
    first, second = iota(square, 0), iota(square, 1)
    ahead = (column < row) | ((column == row) & (first < second))
    place = jnp.sum(jnp.where(ahead, 1.0, 0.0), axis=0, keepdims=True)
    place = jnp.broadcast_to(place, square).T
    half = LANES // 2
    lane_of = jnp.where(first < half, first, half + LANES - 1 - first).astype(F32)
    share = LANES // parts
    rows = []
    for step in range(parts):
        owner_index = lax.bitwise_xor(here, jnp.int32(step))
        target = (owner_index * share + second % share).astype(F32)
        rows.append(jnp.sum(jnp.where(place == target, lane_of, 0.0), axis=0, keepdims=True))
    return jnp.concatenate(rows, axis=0).astype(jnp.int32)


def legendre_kernel(first_unit, units, parts, known, pair_ref, here_ref, owner_ref, s_hbm, l_hbm, *refs):
    if known:
        lanes_ref, outs, refs = owner_ref, refs[:parts], refs[parts:]
    else:
        lanes_ref, outs, refs = refs[parts], refs[:parts], refs[parts + 1 :]
    s_buf, l_buf, table, total, sums, ends, s_sem, l_sem = refs
    _, members, steps, slots, _, length = s_buf.shape
    top = length - 1
    times = members * steps
    rows = 2 * times
    pairs = slots // 2
    unit = pl.program_id(0)
    here = here_ref[0]
    cuts = l_sem.shape[1]
    depth = top // cuts

    def copies(which):
        side = lax.rem(which, 2)
        at = pl.multiple_of((first_unit + which) * slots, slots)
        found = [
            pltpu.make_async_copy(
                s_hbm.at[:, :, pl.ds(at, slots)], s_buf.at[side], s_sem.at[side]
            )
        ]
        at = pl.multiple_of((first_unit + which) * pairs, pairs)
        for cut in range(cuts):
            span = pl.ds(cut * depth, depth if cut < cuts - 1 else length - cut * depth)
            found.append(
                pltpu.make_async_copy(
                    l_hbm.at[span, pl.ds(at, pairs)], l_buf.at[side, span], l_sem.at[side, cut]
                )
            )
        return found

    @pl.when(unit == 0)
    def _():
        for copy in copies(jnp.int32(0)):
            copy.start()
        if not known:
            lanes_ref[...] = latitude_lanes(owner_ref[...], here, parts)

    @pl.when(unit + 1 < units)
    def _():
        for copy in copies(unit + 1):
            copy.start()

    side = lax.rem(unit, 2)
    arriving = copies(unit)
    arriving[0].wait()

    spot = iota((rows, top), 1)
    sign = jnp.where(spot % 2 == 0, 1.0, -1.0).astype(BF16)
    base = here * (pair_ref.shape[0] // parts) + (first_unit + unit) * slots
    for cut in range(cuts):
        arriving[1 + cut].wait()
        for at in range(cut * depth, (cut + 1) * depth, TURN):
            table[:, at : at + TURN, :] = jnp.swapaxes(l_buf[side, at : at + TURN], 0, 1)

    for pair in range(pairs):
        masked = []
        for slot in (2 * pair, 2 * pair + 1):
            x = s_buf[side, :, :, slot].reshape(rows, length)[:, :top]
            first_len = top - pair_ref[base + slot]
            lead = x * jnp.where(spot < first_len, 1.0, 0.0).astype(BF16)
            tail = x - lead
            masked += [lead, lead * sign, tail, tail * sign]
        total[pair] = jnp.dot(
            jnp.concatenate(masked, axis=0), table[pair], preferred_element_type=F32
        )

    low = iota((rows, LANES), 1) < LANES // 2

    ends[...] = l_buf[side, top].astype(F32)

    def combine(pair, carry):
        end = ends[pl.ds(pair, 1), :]
        for odd_slot in range(2):
            slot = 2 * pair + odd_slot
            turned = jnp.where((top - pair_ref[base + slot]) % 2 == 0, 1.0, -1.0).astype(F32)
            last = s_buf[side, :, :, slot, :, top:].reshape(rows, 1).astype(F32) * end
            at = 4 * odd_slot * rows
            north_lead, south_lead, north_tail, south_tail = (
                total[pair, at + i * rows : at + (i + 1) * rows, :] for i in range(4)
            )
            found = (
                (north_lead, south_lead),
                (north_tail + last, (south_tail + last) * turned),
            )
            for which, (north, south) in enumerate(found):
                if odd_slot:
                    both = jnp.where(low, pltpu.roll(north, LANES // 2, 1), south)
                else:
                    both = jnp.where(low, north, pltpu.roll(south, LANES // 2, 1))
                at = pl.multiple_of((2 * slot + which) * rows, rows)
                sums[pl.ds(at, rows), :] = both
        return carry

    [combine(i, 0) for i in range(pairs)]

    waves = 2 * slots
    share = LANES // parts
    per = LANES // share
    group = iota((waves, LANES), 1) // share
    mine = pl.ds(pl.multiple_of(unit * waves, waves), waves)
    for step in range(parts):
        index = jnp.broadcast_to(lanes_ref[step : step + 1, :], (waves, LANES))
        for part in range(2):
            for block in range(times // per):
                built = None
                for place in range(per):
                    at = block * per + place
                    step_of, member = at // members, at % members
                    row = (member * steps + step_of) * 2 + part
                    source = sums[pl.ds(row, waves, stride=rows), :]
                    moved = jnp.take_along_axis(source, index, axis=1, mode="promise_in_bounds")
                    built = moved if place == 0 else jnp.where(group == place, moved, built)
                outs[step][part, mine, block * LANES : (block + 1) * LANES] = built


def legendre_sums(spectra, turned, pair_of_slot, here, owner, first_unit, units, parts):
    members, steps, _, _, length = spectra.shape
    slots = 2 * PAIRS_UNIT
    waves = 2 * slots
    times = members * steps
    width = times * LANES // parts
    known = first_unit > 0
    out = [jax.ShapeDtypeStruct((2, units * waves, width), F32)] * parts
    if not known:
        out = out + [jax.ShapeDtypeStruct((parts, LANES), jnp.int32)]
    here_spec = pl.BlockSpec(memory_space=pltpu.VMEM)
    away = pl.BlockSpec(memory_space=pltpu.HBM)
    return pl.pallas_call(
        functools.partial(legendre_kernel, first_unit, units, parts, known),
        grid_spec=pltpu.PrefetchScalarGridSpec(
            num_scalar_prefetch=2,
            grid=(units,),
            in_specs=[pl.BlockSpec(owner.shape, lambda u, *_: (0, 0)), away, away],
            out_specs=[here_spec] * len(out),
            scratch_shapes=[
                pltpu.VMEM((2, members, steps, slots, 2, length), BF16),
                pltpu.VMEM((2, length, PAIRS_UNIT, LANES), BF16),
                pltpu.VMEM((PAIRS_UNIT, length - 1, LANES), BF16),
                pltpu.VMEM((PAIRS_UNIT, 16 * times, LANES), F32),
                pltpu.VMEM((waves * 2 * times, LANES), F32),
                pltpu.VMEM((PAIRS_UNIT, LANES), F32),
                pltpu.SemaphoreType.DMA((2,)),
                pltpu.SemaphoreType.DMA((2, CUTS)),
            ],
        ),
        out_shape=out,
        compiler_params=pltpu.CompilerParams(vmem_limit_bytes=LEGENDRE_VMEM),
        cost_estimate=pl.CostEstimate(
            flops=units * PAIRS_UNIT * 2 * LANES * LANES * length,
            bytes_accessed=units * PAIRS_UNIT * (LANES + 2 * 2 * times) * length * 2,
            transcendentals=0,
        ),
        name="legendre",
    )(pair_of_slot, here, owner, spectra, turned)


def split(x):
    high = x.astype(BF16)
    return high, (x - high.astype(F32)).astype(BF16)


def turns(numbers, full):
    quarter = full // 4
    turned = (numbers + quarter // 2) // quarter
    x = (numbers - turned * quarter).astype(F32) * (2.0 * math.pi / full)
    y = x * x
    sine = x * (1.0 + y * (-1 / 6 + y * (1 / 120 + y * (-1 / 5040 + y * (1 / 362880)))))
    cosine = 1.0 + y * (-1 / 2 + y * (1 / 24 + y * (-1 / 720 + y * (1 / 40320 - y * (1 / 3628800)))))
    odd = turned % 2 == 1
    c, s = jnp.where(odd, sine, cosine), jnp.where(odd, cosine, sine)
    c = jnp.where((turned == 1) | (turned == 2), -c, c)
    s = jnp.where((turned == 2) | (turned == 3), -s, s)
    return c, s


def tables_kernel(lon, top, waves_ref, coef_ref, t_cos_h, t_cos_l, t_sin_h, t_sin_l, base_ref):
    half, depth = t_cos_h.shape
    coarse = half // NB
    full = 8 * top
    waves = waves_ref[...]
    at = 0
    for factor, shift_by, count in ((2 * NB, 0, coarse), (2, 1, NB)):
        number = factor * iota((count, depth), 0) + shift_by
        c, s = turns(number * waves % full, full)
        base_ref[at : at + count, :] = c
        base_ref[at + count : at + 2 * count, :] = s
        at += 2 * count
    c, s = turns((lon - 1) * waves % full, full)
    rate = waves.astype(F32) * (1.0 / top)
    scale = top ** (-0.5)
    kind = iota((8, depth), 0)
    turn = jnp.where(kind == 0, c * scale, jnp.where(kind == 1, s * scale, rate))
    coef_ref[...] = turn.T

    def fill(a, carry):
        ca = base_ref[pl.ds(a, 1), :]
        sa = base_ref[pl.ds(coarse + a, 1), :]
        cb = base_ref[2 * coarse : 2 * coarse + NB, :]
        sb = base_ref[2 * coarse + NB : 2 * coarse + 2 * NB, :]
        at = pl.ds(pl.multiple_of(a * NB, NB), NB)
        t_cos_h[at, :], t_cos_l[at, :] = split(ca * cb - sa * sb)
        t_sin_h[at, :], t_sin_l[at, :] = split(sa * cb + ca * sb)
        return carry

    lax.fori_loop(0, coarse, fill, 0)


def tables(waves, lon, top):
    depth = waves.shape[1]
    held = pl.BlockSpec(memory_space=pltpu.VMEM)
    out = [jax.ShapeDtypeStruct((depth, 8), F32)]
    out += [jax.ShapeDtypeStruct((lon // 2, depth), BF16)] * 4
    return pl.pallas_call(
        functools.partial(tables_kernel, lon, top),
        in_specs=[held],
        out_specs=[held] * 5,
        out_shape=out,
        scratch_shapes=[pltpu.VMEM((2 * (lon // 2 // NB + NB), depth), F32)],
        compiler_params=pltpu.CompilerParams(vmem_limit_bytes=TABLES_VMEM),
        cost_estimate=pl.CostEstimate(
            flops=16 * lon * depth, bytes_accessed=4 * lon * depth, transcendentals=0
        ),
        name="tables",
    )(waves)


def synthesis_kernel(counts, fresh, closing, shape, *refs):
    lon, regions, wide = shape
    refs = list(refs)
    if closing:
        starts_ref, here_ref = refs.pop(0), refs.pop(0)
    coef_ref, *table_refs = [refs.pop(0) for _ in range(5)]
    pieces = [refs.pop(0) for _ in counts]
    if not fresh:
        cos_in, sin_in = refs.pop(0), refs.pop(0)
    if closing:
        outs = [refs.pop(0) for _ in range(wide)]
    else:
        cos_out, sin_out = refs.pop(0), refs.pop(0)
    w_cos_h, w_cos_l, w_sin_h, w_sin_l = refs[:4]
    step = pl.program_id(0)
    block = lon // 2 // pl.num_programs(0)
    width = pieces[0].shape[2]
    here_rows = pl.ds(pl.multiple_of(step * block, block), block)

    @pl.when(step == 0)
    def _():
        at = 0
        for piece, count in zip(pieces, counts):
            span = slice(at, at + count)
            coef = coef_ref[span, :]
            c, s, rate = coef[:, 0:1], coef[:, 1:2], coef[:, 2:3]
            real, imag = piece[0], piece[1]
            p0 = real * c - imag * s
            p1 = real * s + imag * c
            for index, value in enumerate((p0, rate * p1)):
                cols = slice(index * width, (index + 1) * width)
                w_cos_h[span, cols], w_cos_l[span, cols] = split(value)
            for index, value in enumerate((p1, rate * p0)):
                cols = slice(index * width, (index + 1) * width)
                w_sin_h[span, cols], w_sin_l[span, cols] = split(value)
            at += count

    t_cos_h, t_cos_l, t_sin_h, t_sin_l = (table.at[here_rows, :] for table in table_refs)

    def product(table_h, table_l, weight_h, weight_l):
        dot = functools.partial(jnp.dot, preferred_element_type=F32)
        return (
            dot(table_h[...], weight_h[...])
            + dot(table_l[...], weight_h[...])
            + dot(table_h[...], weight_l[...])
        )

    even = product(t_cos_h, t_cos_l, w_cos_h, w_cos_l)
    odd = product(t_sin_h, t_sin_l, w_sin_h, w_sin_l)
    if not fresh:
        even = even + cos_in[here_rows, :]
        odd = odd + sin_in[here_rows, :]
    if not closing:
        cos_out[here_rows, :] = even
        sin_out[here_rows, :] = odd
        return

    value_ref, slope_ref, found_v, found_s = refs[4:]
    half = lon // 2

    def narrowed(x):
        return functools.reduce(
            jnp.maximum, [x[:, i : i + LANES] for i in range(0, width, LANES)]
        )

    a, d = even[:, :width], even[:, width:]
    b, c = odd[:, :width], odd[:, width:]
    below = pl.ds(pl.multiple_of(step * block, block), block)
    above = pl.ds(pl.multiple_of(half + step * block, block), block)
    value_ref[below, :] = narrowed(a + b)
    value_ref[above, :] = narrowed(a - b)
    slope_ref[below, :] = narrowed(jnp.abs(c - d))
    slope_ref[above, :] = narrowed(jnp.abs(c + d))

    @pl.when(step == pl.num_programs(0) - 1)
    def _():
        window = (WIDEST_REGION + 15) // 8 * 8
        rows = iota((window, LANES), 0)

        def best(low, high):
            at = pl.multiple_of(jnp.minimum(low // 8 * 8, lon - window), 8)
            inside = (rows >= low - at) & (rows < high - at)
            v = jnp.where(inside, value_ref[pl.ds(at, window), :], -3e38)
            s = jnp.where(inside, slope_ref[pl.ds(at, window), :], -3e38)
            return jnp.max(v, axis=0, keepdims=True), jnp.max(s, axis=0, keepdims=True)

        def one(region, carry):
            begin, end = starts_ref[region], starts_ref[region + 1]
            upper = end > half
            low = jnp.where(upper, jnp.maximum(begin, half), half - end)
            high = jnp.where(upper, end, half - begin)
            v, s = best(low, high)
            found_v[pl.ds(region, 1), :] = v
            found_s[pl.ds(region, 1), :] = s
            return carry

        lax.fori_loop(0, regions, one, 0, unroll=8)
        centre = starts_ref[regions + 1]
        v, s = best(0, half - starts_ref[centre])
        at = pl.ds(centre, 1)
        found_v[at, :] = jnp.maximum(found_v[at, :], v)
        found_s[at, :] = jnp.maximum(found_s[at, :], s)
        values, slopes = found_v[...], found_s[...]
        span = LANES
        while span > LANES // 2:
            span //= 2
            values = jnp.maximum(values, pltpu.roll(values, span, 1))
            slopes = jnp.maximum(slopes, pltpu.roll(slopes, span, 1))
        found_v[...] = jnp.where(iota(values.shape, 1) < LANES // 2, values, slopes)
        for offset in range(wide):
            owner = lax.rem(here_ref[0] + offset, wide)
            start = pl.multiple_of(owner * REG_DEV, REG_DEV)
            outs[offset][...] = found_v[pl.ds(start, REG_DEV), :]


def synthesis(made, pieces, held, closing, lon, regions, wide, starts, here):
    block = min(512, lon // 2)
    depth = made[0].shape[0]
    counts = tuple(piece.shape[1] for piece in pieces)
    width = pieces[0].shape[2]
    fresh = held is None
    prefetch = (starts, here) if closing else ()
    operands = [*made, *pieces] + ([] if fresh else list(held))
    in_specs = [pl.BlockSpec(memory_space=pltpu.VMEM)] * len(operands)
    scratch = [pltpu.VMEM((depth, 2 * width), BF16)] * 4
    if closing:
        out_shape = [jax.ShapeDtypeStruct((REG_DEV, LANES), F32)] * wide
        scratch += [pltpu.VMEM((lon, LANES), F32)] * 2 + [pltpu.VMEM((regions, LANES), F32)] * 2
    else:
        out_shape = [jax.ShapeDtypeStruct((lon // 2, 2 * width), F32)] * 2
    out_specs = [pl.BlockSpec(memory_space=pltpu.VMEM)] * len(out_shape)
    return pl.pallas_call(
        functools.partial(
            synthesis_kernel, counts, fresh, closing, (lon, regions, wide)
        ),
        grid_spec=pltpu.PrefetchScalarGridSpec(
            num_scalar_prefetch=len(prefetch),
            grid=(lon // 2 // block,),
            in_specs=in_specs,
            out_specs=out_specs,
            scratch_shapes=scratch,
        ),
        out_shape=out_shape,
        compiler_params=pltpu.CompilerParams(vmem_limit_bytes=SYNTHESIS_VMEM),
        cost_estimate=pl.CostEstimate(
            flops=6 * depth * lon * 2 * width, bytes_accessed=16 * lon * width, transcendentals=0
        ),
        name="synthesis",
    )(*prefetch, *operands)


def shift(x, axis, count, step):
    return lax.ppermute(x, axis, [(i, (i + step) % count) for i in range(count)])


def swap(x, axis, count, step):
    return lax.ppermute(x, axis, [(i, i ^ step) for i in range(count)])


def final_kernel(*refs):
    *found, peak_ref, slope_ref = refs
    best = functools.reduce(jnp.maximum, [x[...] for x in found])
    members, _, share = peak_ref.shape
    for member in range(members):
        peak_ref[member] = best[:, member * share : (member + 1) * share]
        at = LANES // 2 + member * share
        slope_ref[member] = best[:, at : at + share]


def kernels(spectra, legendre, pair_of_slot, lat_owner, region_of_lon):
    members, steps, slot_count, _, length = spectra.shape
    top = length - 1
    lon = region_of_lon.shape[0]
    parts = lax.axis_size("narrow")
    wide = lax.axis_size("wide")
    regions = REG_DEV * wide
    here = lax.axis_index("narrow")
    here_wide = lax.axis_index("wide")
    here_ref = here.reshape(1)
    owner = lat_owner.reshape(1, -1)
    turned = jnp.transpose(legendre, (1, 0, 2))
    tied = lax.optimization_barrier

    kept, beside, near, far, first = [], [], [], [], 0
    for number, units in enumerate(CHUNKS):
        if number >= 1:
            here_ref, kept[-1] = tied((here_ref, kept[-1]))
        if number == 2:
            pair_here, region_of_lon, kept[-1] = tied((pair_of_slot, region_of_lon, kept[-1]))
        if number >= 2:
            here_ref, far[number - 2] = tied((here_ref, far[number - 2]))
        if number >= 3:
            ready = [g for g, group in enumerate(GROUPS) if group[-1] == number - 2]
            for g in ready:
                here_ref, near[g] = tied((here_ref, near[g]))
        sums = legendre_sums(
            spectra, turned, pair_of_slot, here_ref, owner, first, units, parts
        )
        if number == 0:
            owner = sums[parts]
        kept.append(sums[0])
        beside.append(sums[1])
        far.append([swap(sums[i], "narrow", parts, i) for i in range(2, parts)])
        for group in GROUPS:
            if group[-1] == number:
                near.append(swap(jnp.concatenate([beside[i] for i in group], axis=1), "narrow", parts, 1))
        first += units

    waves_of = jnp.stack([pair_here, top - 1 - pair_here], axis=1).reshape(parts, -1)
    waves_of = waves_of[lax.bitwise_xor(here, jnp.arange(parts, dtype=jnp.int32))]
    edges = jnp.arange(regions + 1, dtype=jnp.int32)
    starts = jnp.sum((region_of_lon[None, :] < edges[:, None]).astype(jnp.int32), axis=1)
    starts = jnp.concatenate([starts, region_of_lon[lon // 2 - 1 : lon // 2]])

    per_unit = 4 * PAIRS_UNIT
    bounds = [0]
    for units in CHUNKS:
        bounds.append(bounds[-1] + units * per_unit)

    def piece(array, source, chunks):
        return array, [waves_of[source, bounds[i] : bounds[i + 1]] for i in chunks]

    late = len(CHUNKS) - 1
    own = [piece(kept[i], 0, (i,)) for i in range(late + 1)]
    swapped = [piece(near[g], 1, group) for g, group in enumerate(GROUPS)]
    across = [
        [piece(array, 2 + i, (chunk,)) for i, array in enumerate(far[chunk])]
        for chunk in range(late + 1)
    ]
    stages = (
        own + swapped[:-1] + sum(across[:late], []),
        swapped[-1:] + across[late],
    )
    held = None
    waves = [jnp.concatenate([w for _, found in stage for w in found]) for stage in stages]
    made = [tables(w.reshape(1, -1), lon, top) for w in tied((*waves, kept[-1]))[:-1]]
    for number, stage in enumerate(stages):
        held = synthesis(
            made[number],
            [array for array, _ in stage],
            held,
            number == len(stages) - 1,
            lon,
            regions,
            wide,
            starts,
            here_wide.reshape(1),
        )

    found = [held[0]] + [shift(held[i], "wide", wide, i) for i in range(1, wide)]
    out = jax.ShapeDtypeStruct((members, REG_DEV, LANES // 2 // members), F32)
    peak, peak_slope = pl.pallas_call(
        final_kernel,
        in_specs=[pl.BlockSpec(memory_space=pltpu.VMEM)] * wide,
        out_shape=[out] * 2,
        compiler_params=pltpu.CompilerParams(vmem_limit_bytes=TABLES_VMEM),
        name="final",
    )(*found)
    return jnp.transpose(peak, (0, 2, 1)), jnp.transpose(peak_slope, (0, 2, 1))


def per_device(spectra, legendre, pair_of_slot, lat_owner, region_of_lon):
    members, steps, _, _, length = spectra.shape
    pairs, _, lanes = legendre.shape
    share = lat_owner.shape[0] // lax.axis_size("narrow")
    parts = lax.axis_size("narrow")
    fits = (
        parts & (parts - 1) == 0
        and pairs == PAIRS_UNIT * sum(CHUNKS)
        and lanes == LANES
        and lat_owner.shape[0] == LANES
        and 2 * members * share == LANES
        and members * steps * share % LANES == 0
        and (length - 1) % LANES == 0
        and region_of_lon.shape[0] % 1024 == 0
    )
    run = kernels if fits else plain
    return run(spectra, legendre, pair_of_slot, lat_owner, region_of_lon)


def solution(mesh):
    in_specs = (
        P(None, ("groups", "wide"), "narrow", None, None),
        P("narrow", None, None),
        P(),
        P(),
        P(),
    )
    out_specs = (P("groups", "narrow", "wide"), P("groups", "narrow", "wide"))
    return jax.shard_map(
        per_device, mesh=mesh, in_specs=in_specs, out_specs=out_specs, check_vma=False
    )
```

```python
import functools
import math

import jax
import jax.numpy as jnp
from jax import lax
from jax.experimental import pallas as pl
from jax.experimental.pallas import tpu as pltpu
from jax.sharding import PartitionSpec as P

REG_DEV = 16
WIDEST_REGION = 48
LANES = 128
PAIRS_UNIT = 8
NB = 32
CUTS = 5
LEGENDRE_VMEM = 107 * 2**19
SYNTHESIS_VMEM = 24 * 2**20
TABLES_VMEM = 12 * 2**20
TURN = 128
CHUNKS = (2, 3, 3, 2)
GROUPS = ((0, 1, 2), (3,))
F32 = jnp.float32
BF16 = jnp.bfloat16


def synthesize(operand, waves, start, width, top):
    columns = start + jnp.arange(width, dtype=jnp.int32)
    phase = waves[:, None] * columns[None, :] % (4 * top)
    angle = phase.astype(F32) * (2.0 * math.pi / (4 * top))
    cosine = jnp.cos(angle)
    sine = jnp.sin(angle)
    rate = (waves.astype(F32) / top)[:, None]
    upper = jnp.concatenate([cosine, -rate * sine], axis=1)
    lower = jnp.concatenate([-sine, -rate * cosine], axis=1)
    table = jnp.concatenate([upper, lower], axis=0) * top ** (-0.5)
    return jnp.dot(operand, table, precision=lax.Precision.HIGHEST)


def synthesize_all(operand, waves, lon, top):
    width = min(512, lon)
    starts = jnp.arange(lon // width, dtype=jnp.int32) * width
    blocks = lax.map(lambda begin: synthesize(operand, waves, begin, width, top), starts)
    blocks = blocks.reshape(blocks.shape[0], blocks.shape[1], 2, width)
    value = jnp.transpose(blocks[:, :, 0], (1, 0, 2)).reshape(operand.shape[0], lon)
    slope = jnp.transpose(blocks[:, :, 1], (1, 0, 2)).reshape(operand.shape[0], lon)
    return value, slope


def region_peak(values, region_of_lon, wanted):
    hits = region_of_lon[:, None] == wanted[None, :]
    masked = jnp.where(hits[None, None], values[..., None], -1e30)
    return masked.max(axis=2)


def plain(spectra, legendre, pair_of_slot, lat_owner, region_of_lon):
    members, steps_here, slot_count, _, length = spectra.shape
    top = length - 1
    lon = region_of_lon.shape[0]
    half_count = legendre.shape[0]
    lat_half = legendre.shape[2] // 2
    here = lax.axis_index("narrow")
    paired = lax.dynamic_slice_in_dim(pair_of_slot, here * slot_count, slot_count)
    position = jnp.arange(length, dtype=jnp.int32)[None, :]
    first_len = (top - paired)[:, None]
    leading = position < first_len
    offset = jnp.where(leading, position, position - first_len)
    even_term = offset % 2 == 0
    masks = jnp.stack(
        [leading & even_term, leading & ~even_term, ~leading & even_term, ~leading & ~even_term],
        axis=1,
    ).astype(BF16)
    ordered = jnp.transpose(spectra, (2, 0, 1, 3, 4))
    masked = masks[:, :, None, None, None, :] * ordered[:, None]
    masked = masked.reshape(half_count, 2, -1, length)
    table = legendre.reshape(half_count, length, 2, lat_half)
    sums = jnp.einsum("abrl,albj->abrj", masked, table, preferred_element_type=F32)
    sums = sums.reshape(slot_count, 4, members, steps_here, 2, lat_half)
    north_lead = sums[:, 0] + sums[:, 1]
    south_lead = sums[:, 0] - sums[:, 1]
    north_tail = sums[:, 2] + sums[:, 3]
    south_tail = sums[:, 2] - sums[:, 3]
    lead = jnp.concatenate([north_lead, jnp.flip(south_lead, axis=-1)], axis=-1)
    tail = jnp.concatenate([north_tail, jnp.flip(south_tail, axis=-1)], axis=-1)
    waved = jnp.stack([lead, tail], axis=1).reshape(2 * slot_count, members, steps_here, 2, -1)
    order = jnp.argsort(lat_owner, stable=True)
    waved = jnp.take(waved, order, axis=4)
    arrived = lax.all_to_all(waved, "narrow", split_axis=4, concat_axis=0, tiled=True)
    waves = jnp.stack([pair_of_slot, top - 1 - pair_of_slot], axis=1).reshape(-1)
    lat_here = arrived.shape[4]
    operand = jnp.transpose(arrived, (1, 2, 4, 3, 0)).reshape(members * steps_here * lat_here, -1)
    value, slope = synthesize_all(operand, waves, lon, top)
    value = value.reshape(members, steps_here, lat_here, lon).max(axis=1)
    slope = jnp.abs(slope).reshape(members, steps_here, lat_here, lon).max(axis=1)
    wide_count = lax.axis_size("wide")
    mine_start = lax.axis_index("wide") * REG_DEV
    wanted = jnp.arange(REG_DEV * wide_count, dtype=jnp.int32)
    peaks = region_peak(value, region_of_lon, wanted)
    slopes = region_peak(slope, region_of_lon, wanted)
    peaks, slopes = lax.pmax((peaks, slopes), "wide")
    peak = lax.dynamic_slice_in_dim(peaks, mine_start, REG_DEV, 2)
    peak_slope = lax.dynamic_slice_in_dim(slopes, mine_start, REG_DEV, 2)
    return peak, peak_slope


def iota(shape, axis):
    return lax.broadcasted_iota(jnp.int32, shape, axis)


def latitude_lanes(owner, here, parts, members, steps):
    square = (LANES, LANES)
    row = jnp.broadcast_to(owner.astype(F32), square)
    column = row.T
    first, second = iota(square, 0), iota(square, 1)
    ahead = (column < row) | ((column == row) & (first < second))
    place = jnp.sum(jnp.where(ahead, 1.0, 0.0), axis=0, keepdims=True)
    place = jnp.broadcast_to(place, square).T
    half = LANES // 2
    lane_of = jnp.where(first < half, first, half + LANES - 1 - first).astype(F32)
    share = LANES // parts
    shape = (2 * members * steps, LANES)
    at = iota(shape, 0) // 2
    at = at % steps * members + at // steps
    relative = lax.bitwise_xor(iota(shape, 1) // share, at % parts)
    lanes = jnp.zeros(shape, F32)
    for step in range(parts):
        owner_index = lax.bitwise_xor(here, jnp.int32(step))
        target = (owner_index * share + second % share).astype(F32)
        found = jnp.sum(jnp.where(place == target, lane_of, 0.0), axis=0, keepdims=True)
        lanes = jnp.where(relative == step, found, lanes)
    return lanes.astype(jnp.int32)


def legendre_kernel(first_unit, units, parts, known, pair_ref, here_ref, owner_ref, s_hbm, l_hbm, *refs):
    if known:
        lanes_ref, outs, refs = owner_ref, refs[:parts], refs[parts:]
    else:
        lanes_ref, outs, refs = refs[parts], refs[:parts], refs[parts + 1 :]
    s_buf, l_buf, table, total, sums, ends, s_sem, l_sem = refs
    _, members, steps, slots, _, length = s_buf.shape
    top = length - 1
    times = members * steps
    rows = 2 * times
    pairs = slots // 2
    unit = pl.program_id(0)
    here = here_ref[0]
    cuts = l_sem.shape[1]
    depth = top // cuts

    def copies(which):
        side = lax.rem(which, 2)
        found = []
        at = pl.multiple_of((first_unit + which) * pairs, pairs)
        for cut in range(cuts):
            span = pl.ds(cut * depth, depth if cut < cuts - 1 else length - cut * depth)
            found.append(
                pltpu.make_async_copy(
                    l_hbm.at[span, pl.ds(at, pairs)], l_buf.at[side, span], l_sem.at[side, cut]
                )
            )
        at = pl.multiple_of((first_unit + which) * slots, slots)
        found.append(
            pltpu.make_async_copy(
                s_hbm.at[:, :, pl.ds(at, slots)], s_buf.at[side], s_sem.at[side]
            )
        )
        return found

    @pl.when(unit == 0)
    def _():
        for copy in copies(jnp.int32(0)):
            copy.start()
        if not known:
            lanes_ref[...] = latitude_lanes(owner_ref[...], here, parts, members, steps)

    @pl.when(unit + 1 < units)
    def _():
        for copy in copies(unit + 1):
            copy.start()

    side = lax.rem(unit, 2)
    arriving = copies(unit)

    spot = iota((8, top), 1)
    sign = jnp.where(iota((rows, top), 1) % 2 == 0, 1.0, -1.0).astype(BF16)
    base = here * (pair_ref.shape[0] // parts) + (first_unit + unit) * slots
    for cut in range(cuts):
        arriving[cut].wait()
        for at in range(cut * depth, (cut + 1) * depth, TURN):
            table[:, at : at + TURN, :] = jnp.swapaxes(l_buf[side, at : at + TURN], 0, 1)

    arriving[cuts].wait()
    for pair in range(pairs):
        masked = []
        for slot in (2 * pair, 2 * pair + 1):
            x = s_buf[side, :, :, slot].reshape(rows, length)[:, :top]
            first_len = top - pair_ref[base + slot]
            inside = jnp.where(spot < first_len, 1.0, 0.0)
            lead = x * jnp.concatenate([inside] * (rows // 8), axis=0).astype(BF16)
            masked += [lead, lead * sign, x, x * sign]
        total[pair] = jnp.dot(
            jnp.concatenate(masked, axis=0), table[pair], preferred_element_type=F32
        )

    low = iota((rows, LANES), 1) < LANES // 2

    ends[...] = l_buf[side, top].astype(F32)
    lanes = lanes_ref[...]

    def combine(pair, carry):
        end = ends[pl.ds(pair, 1), :]
        for odd_slot in range(2):
            slot = 2 * pair + odd_slot
            turned = jnp.where((top - pair_ref[base + slot]) % 2 == 0, 1.0, -1.0).astype(F32)
            last = s_buf[side, :, :, slot, :, top:].reshape(rows, 1).astype(F32) * end
            at = 4 * odd_slot * rows
            north_lead, south_lead, north, south = (
                total[pair, at + i * rows : at + (i + 1) * rows, :] for i in range(4)
            )
            found = (
                (north_lead, south_lead),
                (north - north_lead + last, (south - south_lead + last) * turned),
            )
            for which, (north, south) in enumerate(found):
                if odd_slot:
                    both = jnp.where(low, pltpu.roll(north, LANES // 2, 1), south)
                else:
                    both = jnp.where(low, north, pltpu.roll(south, LANES // 2, 1))
                at = pl.multiple_of((2 * slot + which) * rows, rows)
                sums[pl.ds(at, rows), :] = jnp.take_along_axis(
                    both, lanes, axis=1, mode="promise_in_bounds"
                )
        return carry

    [combine(i, 0) for i in range(pairs)]

    waves = 2 * slots
    share = LANES // parts
    per = LANES // share
    group = iota((waves, LANES), 1) // share
    mine = pl.ds(pl.multiple_of(unit * waves, waves), waves)
    for part in range(2):
        for block in range(times // per):
            sources = []
            for place in range(per):
                step_of, member = (block * per + place) // members, (block * per + place) % members
                row = (member * steps + step_of) * 2 + part
                sources.append(sums[pl.ds(row, waves, stride=rows), :])
            for step in range(parts):
                built = sources[step]
                for place in range(1, per):
                    built = jnp.where(group == place, sources[place ^ step], built)
                outs[step][part, mine, block * LANES : (block + 1) * LANES] = built


def legendre_sums(spectra, turned, pair_of_slot, here, owner, first_unit, units, parts):
    members, steps, _, _, length = spectra.shape
    slots = 2 * PAIRS_UNIT
    waves = 2 * slots
    times = members * steps
    width = times * LANES // parts
    known = first_unit > 0
    out = [jax.ShapeDtypeStruct((2, units * waves, width), F32)] * parts
    if not known:
        out = out + [jax.ShapeDtypeStruct((2 * times, LANES), jnp.int32)]
    here_spec = pl.BlockSpec(memory_space=pltpu.VMEM)
    away = pl.BlockSpec(memory_space=pltpu.HBM)
    return pl.pallas_call(
        functools.partial(legendre_kernel, first_unit, units, parts, known),
        grid_spec=pltpu.PrefetchScalarGridSpec(
            num_scalar_prefetch=2,
            grid=(units,),
            in_specs=[pl.BlockSpec(owner.shape, lambda u, *_: (0, 0)), away, away],
            out_specs=[here_spec] * len(out),
            scratch_shapes=[
                pltpu.VMEM((2, members, steps, slots, 2, length), BF16),
                pltpu.VMEM((2, length, PAIRS_UNIT, LANES), BF16),
                pltpu.VMEM((PAIRS_UNIT, length - 1, LANES), BF16),
                pltpu.VMEM((PAIRS_UNIT, 16 * times, LANES), F32),
                pltpu.VMEM((waves * 2 * times, LANES), F32),
                pltpu.VMEM((PAIRS_UNIT, LANES), F32),
                pltpu.SemaphoreType.DMA((2,)),
                pltpu.SemaphoreType.DMA((2, CUTS)),
            ],
        ),
        out_shape=out,
        compiler_params=pltpu.CompilerParams(vmem_limit_bytes=LEGENDRE_VMEM),
        cost_estimate=pl.CostEstimate(
            flops=units * PAIRS_UNIT * 2 * LANES * LANES * length,
            bytes_accessed=units * PAIRS_UNIT * (LANES + 2 * 2 * times) * length * 2,
            transcendentals=0,
        ),
        name="legendre",
    )(pair_of_slot, here, owner, spectra, turned)


def split(x):
    high = x.astype(BF16)
    return high, (x - high.astype(F32)).astype(BF16)


def turns(numbers, full):
    quarter = full // 4
    turned = (numbers + quarter // 2) // quarter
    x = (numbers - turned * quarter).astype(F32) * (2.0 * math.pi / full)
    y = x * x
    sine = x * (1.0 + y * (-1 / 6 + y * (1 / 120 + y * (-1 / 5040 + y * (1 / 362880)))))
    cosine = 1.0 + y * (-1 / 2 + y * (1 / 24 + y * (-1 / 720 + y * (1 / 40320 - y * (1 / 3628800)))))
    odd = turned % 2 == 1
    c, s = jnp.where(odd, sine, cosine), jnp.where(odd, cosine, sine)
    c = jnp.where((turned == 1) | (turned == 2), -c, c)
    s = jnp.where((turned == 2) | (turned == 3), -s, s)
    return c, s


def regrouped(x, step, share):
    if step == 0:
        return x
    shape = (x.shape[0], LANES)
    index = lax.bitwise_xor(iota(shape, 1), jnp.int32(step * share))
    return jnp.concatenate(
        [
            jnp.take_along_axis(x[:, i : i + LANES], index, axis=1, mode="promise_in_bounds")
            for i in range(0, x.shape[1], LANES)
        ],
        axis=1,
    )


def tables_kernel(lon, top, waves_ref, coef_ref, t_cos_h, t_cos_l, t_sin_h, t_sin_l, base_ref):
    half, depth = t_cos_h.shape
    coarse = half // NB
    full = 8 * top
    waves = waves_ref[...]
    at = 0
    for factor, shift_by, count in ((2 * NB, 0, coarse), (2, 1, NB)):
        number = factor * iota((count, depth), 0) + shift_by
        c, s = turns(number * waves % full, full)
        base_ref[at : at + count, :] = c
        base_ref[at + count : at + 2 * count, :] = s
        at += 2 * count
    c, s = turns((lon - 1) * waves % full, full)
    rate = waves.astype(F32) * (1.0 / top)
    scale = top ** (-0.5)
    kind = iota((8, depth), 0)
    turn = jnp.where(kind == 0, c * scale, jnp.where(kind == 1, s * scale, rate))
    coef_ref[...] = turn.T

    def fill(a, carry):
        ca = base_ref[pl.ds(a, 1), :]
        sa = base_ref[pl.ds(coarse + a, 1), :]
        cb = base_ref[2 * coarse : 2 * coarse + NB, :]
        sb = base_ref[2 * coarse + NB : 2 * coarse + 2 * NB, :]
        at = pl.ds(pl.multiple_of(a * NB, NB), NB)
        t_cos_h[at, :], t_cos_l[at, :] = split(ca * cb - sa * sb)
        t_sin_h[at, :], t_sin_l[at, :] = split(sa * cb + ca * sb)
        return carry

    lax.fori_loop(0, coarse, fill, 0)


def tables(waves, lon, top):
    depth = waves.shape[1]
    held = pl.BlockSpec(memory_space=pltpu.VMEM)
    out = [jax.ShapeDtypeStruct((depth, 8), F32)]
    out += [jax.ShapeDtypeStruct((lon // 2, depth), BF16)] * 4
    return pl.pallas_call(
        functools.partial(tables_kernel, lon, top),
        in_specs=[held],
        out_specs=[held] * 5,
        out_shape=out,
        scratch_shapes=[pltpu.VMEM((2 * (lon // 2 // NB + NB), depth), F32)],
        compiler_params=pltpu.CompilerParams(vmem_limit_bytes=TABLES_VMEM),
        cost_estimate=pl.CostEstimate(
            flops=16 * lon * depth, bytes_accessed=4 * lon * depth, transcendentals=0
        ),
        name="tables",
    )(waves)


def synthesis_kernel(counts, fresh, closing, shape, *refs):
    lon, regions, wide, share = shape
    refs = list(refs)
    if closing:
        starts_ref, here_ref = refs.pop(0), refs.pop(0)
    coef_ref, *table_refs = [refs.pop(0) for _ in range(5)]
    pieces = [refs.pop(0) for _ in counts]
    if not fresh:
        cos_in, sin_in = refs.pop(0), refs.pop(0)
    if closing:
        outs = [refs.pop(0) for _ in range(wide)]
    else:
        cos_out, sin_out = refs.pop(0), refs.pop(0)
    w_cos_h, w_cos_l, w_sin_h, w_sin_l = refs[:4]
    step = pl.program_id(0)
    block = lon // 2 // pl.num_programs(0)
    width = pieces[0].shape[2]
    here_rows = pl.ds(pl.multiple_of(step * block, block), block)

    @pl.when(step == 0)
    def _():
        at = 0
        for piece, (count, step_of) in zip(pieces, counts):
            span = slice(at, at + count)
            coef = coef_ref[span, :]
            c, s, rate = coef[:, 0:1], coef[:, 1:2], coef[:, 2:3]
            real, imag = (regrouped(piece[i], step_of, share) for i in range(2))
            p0 = real * c - imag * s
            p1 = real * s + imag * c
            for index, value in enumerate((p0, rate * p1)):
                cols = slice(index * width, (index + 1) * width)
                w_cos_h[span, cols], w_cos_l[span, cols] = split(value)
            for index, value in enumerate((p1, rate * p0)):
                cols = slice(index * width, (index + 1) * width)
                w_sin_h[span, cols], w_sin_l[span, cols] = split(value)
            at += count

    t_cos_h, t_cos_l, t_sin_h, t_sin_l = (table.at[here_rows, :] for table in table_refs)

    def product(table_h, table_l, weight_h, weight_l):
        dot = functools.partial(jnp.dot, preferred_element_type=F32)
        return (
            dot(table_h[...], weight_h[...])
            + dot(table_l[...], weight_h[...])
            + dot(table_h[...], weight_l[...])
        )

    even = product(t_cos_h, t_cos_l, w_cos_h, w_cos_l)
    odd = product(t_sin_h, t_sin_l, w_sin_h, w_sin_l)
    if not fresh:
        even = even + cos_in[here_rows, :]
        odd = odd + sin_in[here_rows, :]
    if not closing:
        cos_out[here_rows, :] = even
        sin_out[here_rows, :] = odd
        return

    value_ref, slope_ref, found_v, found_s = refs[4:]
    half = lon // 2

    def narrowed(x):
        return functools.reduce(
            jnp.maximum, [x[:, i : i + LANES] for i in range(0, width, LANES)]
        )

    a, d = even[:, :width], even[:, width:]
    b, c = odd[:, :width], odd[:, width:]
    below = pl.ds(pl.multiple_of(step * block, block), block)
    above = pl.ds(pl.multiple_of(half + step * block, block), block)
    value_ref[below, :] = narrowed(a + b)
    value_ref[above, :] = narrowed(a - b)
    slope_ref[below, :] = narrowed(jnp.abs(c - d))
    slope_ref[above, :] = narrowed(jnp.abs(c + d))

    @pl.when(step == pl.num_programs(0) - 1)
    def _():
        window = (WIDEST_REGION + 15) // 8 * 8
        rows = iota((window, LANES), 0)

        def best(low, high):
            at = pl.multiple_of(jnp.minimum(low // 8 * 8, lon - window), 8)
            inside = (rows >= low - at) & (rows < high - at)
            v = jnp.where(inside, value_ref[pl.ds(at, window), :], -3e38)
            s = jnp.where(inside, slope_ref[pl.ds(at, window), :], -3e38)
            return jnp.max(v, axis=0, keepdims=True), jnp.max(s, axis=0, keepdims=True)

        def one(region, carry):
            begin, end = starts_ref[region], starts_ref[region + 1]
            upper = end > half
            low = jnp.where(upper, jnp.maximum(begin, half), half - end)
            high = jnp.where(upper, end, half - begin)
            v, s = best(low, high)
            found_v[pl.ds(region, 1), :] = v
            found_s[pl.ds(region, 1), :] = s
            return carry

        lax.fori_loop(0, regions, one, 0, unroll=8)
        centre = starts_ref[regions + 1]
        v, s = best(0, half - starts_ref[centre])
        at = pl.ds(centre, 1)
        found_v[at, :] = jnp.maximum(found_v[at, :], v)
        found_s[at, :] = jnp.maximum(found_s[at, :], s)
        values, slopes = found_v[...], found_s[...]
        span = LANES
        while span > LANES // 2:
            span //= 2
            values = jnp.maximum(values, pltpu.roll(values, span, 1))
            slopes = jnp.maximum(slopes, pltpu.roll(slopes, span, 1))
        found_v[...] = jnp.where(iota(values.shape, 1) < LANES // 2, values, slopes)
        for offset in range(wide):
            owner = lax.rem(here_ref[0] + offset, wide)
            start = pl.multiple_of(owner * REG_DEV, REG_DEV)
            outs[offset][...] = found_v[pl.ds(start, REG_DEV), :]


def synthesis(made, pieces, sources, held, closing, lon, regions, wide, share, starts, here):
    block = min(512, lon // 2)
    depth = made[0].shape[0]
    counts = tuple((piece.shape[1], source) for piece, source in zip(pieces, sources))
    width = pieces[0].shape[2]
    fresh = held is None
    prefetch = (starts, here) if closing else ()
    operands = [*made, *pieces] + ([] if fresh else list(held))
    in_specs = [pl.BlockSpec(memory_space=pltpu.VMEM)] * len(operands)
    scratch = [pltpu.VMEM((depth, 2 * width), BF16)] * 4
    if closing:
        out_shape = [jax.ShapeDtypeStruct((REG_DEV, LANES), F32)] * wide
        scratch += [pltpu.VMEM((lon, LANES), F32)] * 2 + [pltpu.VMEM((regions, LANES), F32)] * 2
    else:
        out_shape = [jax.ShapeDtypeStruct((lon // 2, 2 * width), F32)] * 2
    out_specs = [pl.BlockSpec(memory_space=pltpu.VMEM)] * len(out_shape)
    return pl.pallas_call(
        functools.partial(
            synthesis_kernel, counts, fresh, closing, (lon, regions, wide, share)
        ),
        grid_spec=pltpu.PrefetchScalarGridSpec(
            num_scalar_prefetch=len(prefetch),
            grid=(lon // 2 // block,),
            in_specs=in_specs,
            out_specs=out_specs,
            scratch_shapes=scratch,
        ),
        out_shape=out_shape,
        compiler_params=pltpu.CompilerParams(vmem_limit_bytes=SYNTHESIS_VMEM),
        cost_estimate=pl.CostEstimate(
            flops=6 * depth * lon * 2 * width, bytes_accessed=16 * lon * width, transcendentals=0
        ),
        name="synthesis",
    )(*prefetch, *operands)


def shift(x, axis, count, step):
    return lax.ppermute(x, axis, [(i, (i + step) % count) for i in range(count)])


def swap(x, axis, count, step):
    return lax.ppermute(x, axis, [(i, i ^ step) for i in range(count)])


def final_kernel(*refs):
    *found, peak_ref, slope_ref = refs
    best = functools.reduce(jnp.maximum, [x[...] for x in found])
    members, _, share = peak_ref.shape
    for member in range(members):
        peak_ref[member] = best[:, member * share : (member + 1) * share]
        at = LANES // 2 + member * share
        slope_ref[member] = best[:, at : at + share]


def kernels(spectra, legendre, pair_of_slot, lat_owner, region_of_lon):
    members, steps, slot_count, _, length = spectra.shape
    top = length - 1
    lon = region_of_lon.shape[0]
    parts = lax.axis_size("narrow")
    wide = lax.axis_size("wide")
    regions = REG_DEV * wide
    here = lax.axis_index("narrow")
    here_wide = lax.axis_index("wide")
    here_ref = here.reshape(1)
    owner = lat_owner.reshape(1, -1)
    turned = jnp.transpose(legendre, (1, 0, 2))
    tied = lax.optimization_barrier

    kept, beside, near, far, first = [], [], [], [], 0
    for number, units in enumerate(CHUNKS):
        if number >= 1:
            here_ref, kept[-1] = tied((here_ref, kept[-1]))
        if number == 2:
            pair_here, region_of_lon, kept[-1] = tied((pair_of_slot, region_of_lon, kept[-1]))
        if number >= 2:
            here_ref, far[number - 2] = tied((here_ref, far[number - 2]))
        if number >= 3:
            ready = [g for g, group in enumerate(GROUPS) if group[-1] == number - 2]
            for g in ready:
                here_ref, near[g] = tied((here_ref, near[g]))
        sums = legendre_sums(
            spectra, turned, pair_of_slot, here_ref, owner, first, units, parts
        )
        if number == 0:
            owner = sums[parts]
        kept.append(sums[0])
        beside.append(sums[1])
        far.append([swap(sums[i], "narrow", parts, i) for i in range(2, parts)])
        for group in GROUPS:
            if group[-1] == number:
                near.append(swap(jnp.concatenate([beside[i] for i in group], axis=1), "narrow", parts, 1))
        first += units

    waves_of = jnp.stack([pair_here, top - 1 - pair_here], axis=1).reshape(parts, -1)
    waves_of = waves_of[lax.bitwise_xor(here, jnp.arange(parts, dtype=jnp.int32))]
    edges = jnp.arange(regions + 1, dtype=jnp.int32)
    starts = jnp.sum((region_of_lon[None, :] < edges[:, None]).astype(jnp.int32), axis=1)
    starts = jnp.concatenate([starts, region_of_lon[lon // 2 - 1 : lon // 2]])

    per_unit = 4 * PAIRS_UNIT
    bounds = [0]
    for units in CHUNKS:
        bounds.append(bounds[-1] + units * per_unit)

    def piece(array, source, chunks):
        return array, source, [waves_of[source, bounds[i] : bounds[i + 1]] for i in chunks]

    late = len(CHUNKS) - 1
    own = [piece(kept[i], 0, (i,)) for i in range(late + 1)]
    swapped = [piece(near[g], 1, group) for g, group in enumerate(GROUPS)]
    across = [
        [piece(array, 2 + i, (chunk,)) for i, array in enumerate(far[chunk])]
        for chunk in range(late + 1)
    ]
    stages = (
        own + swapped[:-1] + sum(across[:late], []),
        swapped[-1:] + across[late],
    )
    held = None
    waves = [jnp.concatenate([w for _, _, found in stage for w in found]) for stage in stages]
    made = [tables(w.reshape(1, -1), lon, top) for w in tied((*waves, kept[-1]))[:-1]]
    for number, stage in enumerate(stages):
        held = synthesis(
            made[number],
            [array for array, _, _ in stage],
            [source for _, source, _ in stage],
            held,
            number == len(stages) - 1,
            lon,
            regions,
            wide,
            LANES // parts,
            starts,
            here_wide.reshape(1),
        )

    found = [held[0]] + [shift(held[i], "wide", wide, i) for i in range(1, wide)]
    out = jax.ShapeDtypeStruct((members, REG_DEV, LANES // 2 // members), F32)
    peak, peak_slope = pl.pallas_call(
        final_kernel,
        in_specs=[pl.BlockSpec(memory_space=pltpu.VMEM)] * wide,
        out_shape=[out] * 2,
        compiler_params=pltpu.CompilerParams(vmem_limit_bytes=TABLES_VMEM),
        name="final",
    )(*found)
    return jnp.transpose(peak, (0, 2, 1)), jnp.transpose(peak_slope, (0, 2, 1))


def per_device(spectra, legendre, pair_of_slot, lat_owner, region_of_lon):
    members, steps, _, _, length = spectra.shape
    pairs, _, lanes = legendre.shape
    share = lat_owner.shape[0] // lax.axis_size("narrow")
    parts = lax.axis_size("narrow")
    fits = (
        parts & (parts - 1) == 0
        and pairs == PAIRS_UNIT * sum(CHUNKS)
        and lanes == LANES
        and lat_owner.shape[0] == LANES
        and 2 * members * share == LANES
        and members * steps * share % LANES == 0
        and (length - 1) % LANES == 0
        and region_of_lon.shape[0] % 1024 == 0
    )
    run = kernels if fits else plain
    return run(spectra, legendre, pair_of_slot, lat_owner, region_of_lon)


def solution(mesh):
    in_specs = (
        P(None, ("groups", "wide"), "narrow", None, None),
        P("narrow", None, None),
        P(),
        P(),
        P(),
    )
    out_specs = (P("groups", "narrow", "wide"), P("groups", "narrow", "wide"))
    return jax.shard_map(
        per_device, mesh=mesh, in_specs=in_specs, out_specs=out_specs, check_vma=False
    )
```

```python
import functools
import math

import jax
import jax.numpy as jnp
from jax import lax
from jax.experimental import pallas as pl
from jax.experimental.pallas import tpu as pltpu
from jax.sharding import PartitionSpec as P

REG_DEV = 16
WIDEST_REGION = 48
LANES = 128
PAIRS_UNIT = 8
NB = 32
CUTS = 5
LEGENDRE_VMEM = 107 * 2**19
SYNTHESIS_VMEM = 24 * 2**20
TABLES_VMEM = 12 * 2**20
TURN = 128
CHUNKS = (2, 3, 3, 2)
GROUPS = ((0, 1, 2), (3,))
F32 = jnp.float32
BF16 = jnp.bfloat16


def synthesize(operand, waves, start, width, top):
    columns = start + jnp.arange(width, dtype=jnp.int32)
    phase = waves[:, None] * columns[None, :] % (4 * top)
    angle = phase.astype(F32) * (2.0 * math.pi / (4 * top))
    cosine = jnp.cos(angle)
    sine = jnp.sin(angle)
    rate = (waves.astype(F32) / top)[:, None]
    upper = jnp.concatenate([cosine, -rate * sine], axis=1)
    lower = jnp.concatenate([-sine, -rate * cosine], axis=1)
    table = jnp.concatenate([upper, lower], axis=0) * top ** (-0.5)
    return jnp.dot(operand, table, precision=lax.Precision.HIGHEST)


def synthesize_all(operand, waves, lon, top):
    width = min(512, lon)
    starts = jnp.arange(lon // width, dtype=jnp.int32) * width
    blocks = lax.map(lambda begin: synthesize(operand, waves, begin, width, top), starts)
    blocks = blocks.reshape(blocks.shape[0], blocks.shape[1], 2, width)
    value = jnp.transpose(blocks[:, :, 0], (1, 0, 2)).reshape(operand.shape[0], lon)
    slope = jnp.transpose(blocks[:, :, 1], (1, 0, 2)).reshape(operand.shape[0], lon)
    return value, slope


def region_peak(values, region_of_lon, wanted):
    hits = region_of_lon[:, None] == wanted[None, :]
    masked = jnp.where(hits[None, None], values[..., None], -1e30)
    return masked.max(axis=2)


def plain(spectra, legendre, pair_of_slot, lat_owner, region_of_lon):
    members, steps_here, slot_count, _, length = spectra.shape
    top = length - 1
    lon = region_of_lon.shape[0]
    half_count = legendre.shape[0]
    lat_half = legendre.shape[2] // 2
    here = lax.axis_index("narrow")
    paired = lax.dynamic_slice_in_dim(pair_of_slot, here * slot_count, slot_count)
    position = jnp.arange(length, dtype=jnp.int32)[None, :]
    first_len = (top - paired)[:, None]
    leading = position < first_len
    offset = jnp.where(leading, position, position - first_len)
    even_term = offset % 2 == 0
    masks = jnp.stack(
        [leading & even_term, leading & ~even_term, ~leading & even_term, ~leading & ~even_term],
        axis=1,
    ).astype(BF16)
    ordered = jnp.transpose(spectra, (2, 0, 1, 3, 4))
    masked = masks[:, :, None, None, None, :] * ordered[:, None]
    masked = masked.reshape(half_count, 2, -1, length)
    table = legendre.reshape(half_count, length, 2, lat_half)
    sums = jnp.einsum("abrl,albj->abrj", masked, table, preferred_element_type=F32)
    sums = sums.reshape(slot_count, 4, members, steps_here, 2, lat_half)
    north_lead = sums[:, 0] + sums[:, 1]
    south_lead = sums[:, 0] - sums[:, 1]
    north_tail = sums[:, 2] + sums[:, 3]
    south_tail = sums[:, 2] - sums[:, 3]
    lead = jnp.concatenate([north_lead, jnp.flip(south_lead, axis=-1)], axis=-1)
    tail = jnp.concatenate([north_tail, jnp.flip(south_tail, axis=-1)], axis=-1)
    waved = jnp.stack([lead, tail], axis=1).reshape(2 * slot_count, members, steps_here, 2, -1)
    order = jnp.argsort(lat_owner, stable=True)
    waved = jnp.take(waved, order, axis=4)
    arrived = lax.all_to_all(waved, "narrow", split_axis=4, concat_axis=0, tiled=True)
    waves = jnp.stack([pair_of_slot, top - 1 - pair_of_slot], axis=1).reshape(-1)
    lat_here = arrived.shape[4]
    operand = jnp.transpose(arrived, (1, 2, 4, 3, 0)).reshape(members * steps_here * lat_here, -1)
    value, slope = synthesize_all(operand, waves, lon, top)
    value = value.reshape(members, steps_here, lat_here, lon).max(axis=1)
    slope = jnp.abs(slope).reshape(members, steps_here, lat_here, lon).max(axis=1)
    wide_count = lax.axis_size("wide")
    mine_start = lax.axis_index("wide") * REG_DEV
    wanted = jnp.arange(REG_DEV * wide_count, dtype=jnp.int32)
    peaks = region_peak(value, region_of_lon, wanted)
    slopes = region_peak(slope, region_of_lon, wanted)
    peaks, slopes = lax.pmax((peaks, slopes), "wide")
    peak = lax.dynamic_slice_in_dim(peaks, mine_start, REG_DEV, 2)
    peak_slope = lax.dynamic_slice_in_dim(slopes, mine_start, REG_DEV, 2)
    return peak, peak_slope


def iota(shape, axis):
    return lax.broadcasted_iota(jnp.int32, shape, axis)


def latitude_lanes(owner, here, parts, members, steps):
    square = (LANES, LANES)
    row = jnp.broadcast_to(owner.astype(F32), square)
    column = row.T
    first, second = iota(square, 0), iota(square, 1)
    ahead = (column < row) | ((column == row) & (first < second))
    place = jnp.sum(jnp.where(ahead, 1.0, 0.0), axis=0, keepdims=True)
    place = jnp.broadcast_to(place, square).T
    half = LANES // 2
    lane_of = jnp.where(first < half, first, half + LANES - 1 - first).astype(F32)
    share = LANES // parts
    shape = (2 * members * steps, LANES)
    at = iota(shape, 0) // 2
    at = at % steps * members + at // steps
    relative = lax.bitwise_xor(iota(shape, 1) // share, at % parts)
    lanes = jnp.zeros(shape, F32)
    for step in range(parts):
        owner_index = lax.bitwise_xor(here, jnp.int32(step))
        target = (owner_index * share + second % share).astype(F32)
        found = jnp.sum(jnp.where(place == target, lane_of, 0.0), axis=0, keepdims=True)
        lanes = jnp.where(relative == step, found, lanes)
    return lanes.astype(jnp.int32)


def legendre_kernel(first_unit, units, parts, known, pair_ref, here_ref, owner_ref, s_hbm, l_hbm, *refs):
    if known:
        lanes_ref, outs, refs = owner_ref, refs[:parts], refs[parts:]
    else:
        lanes_ref, outs, refs = refs[parts], refs[:parts], refs[parts + 1 :]
    s_buf, l_buf, table, total, sums, ends, s_sem, l_sem = refs
    _, members, steps, slots, _, length = s_buf.shape
    top = length - 1
    times = members * steps
    rows = 2 * times
    pairs = slots // 2
    unit = pl.program_id(0)
    here = here_ref[0]
    cuts = l_sem.shape[1]
    depth = top // cuts

    def copies(which):
        side = lax.rem(which, 2)
        found = []
        at = pl.multiple_of((first_unit + which) * pairs, pairs)
        for cut in range(cuts):
            span = pl.ds(cut * depth, depth if cut < cuts - 1 else length - cut * depth)
            found.append(
                pltpu.make_async_copy(
                    l_hbm.at[span, pl.ds(at, pairs)], l_buf.at[side, span], l_sem.at[side, cut]
                )
            )
        at = pl.multiple_of((first_unit + which) * slots, slots)
        found.append(
            pltpu.make_async_copy(
                s_hbm.at[:, :, pl.ds(at, slots)], s_buf.at[side], s_sem.at[side]
            )
        )
        return found

    @pl.when(unit == 0)
    def _():
        for copy in copies(jnp.int32(0)):
            copy.start()
        if not known:
            lanes_ref[...] = latitude_lanes(owner_ref[...], here, parts, members, steps)

    @pl.when(unit + 1 < units)
    def _():
        for copy in copies(unit + 1):
            copy.start()

    side = lax.rem(unit, 2)
    arriving = copies(unit)

    spot = iota((8, top), 1)
    sign = jnp.where(iota((rows, top), 1) % 2 == 0, 1.0, -1.0).astype(BF16)
    base = here * (pair_ref.shape[0] // parts) + (first_unit + unit) * slots
    for cut in range(cuts):
        arriving[cut].wait()
        for at in range(cut * depth, (cut + 1) * depth, TURN):
            table[:, at : at + TURN, :] = jnp.swapaxes(l_buf[side, at : at + TURN], 0, 1)

    arriving[cuts].wait()
    for pair in range(pairs):
        masked = []
        for slot in (2 * pair, 2 * pair + 1):
            x = s_buf[side, :, :, slot].reshape(rows, length)[:, :top]
            first_len = top - pair_ref[base + slot]
            inside = jnp.where(spot < first_len, 1.0, 0.0)
            lead = x * jnp.concatenate([inside] * (rows // 8), axis=0).astype(BF16)
            masked += [lead, lead * sign, x, x * sign]
        total[pair] = jnp.dot(
            jnp.concatenate(masked, axis=0), table[pair], preferred_element_type=F32
        )

    low = iota((rows, LANES), 1) < LANES // 2

    ends[...] = l_buf[side, top].astype(F32)
    lanes = lanes_ref[...]

    def combine(pair, carry):
        end = ends[pl.ds(pair, 1), :]
        for odd_slot in range(2):
            slot = 2 * pair + odd_slot
            turned = jnp.where((top - pair_ref[base + slot]) % 2 == 0, 1.0, -1.0).astype(F32)
            last = s_buf[side, :, :, slot, :, top:].reshape(rows, 1).astype(F32) * end
            at = 4 * odd_slot * rows
            north_lead, south_lead, north, south = (
                total[pair, at + i * rows : at + (i + 1) * rows, :] for i in range(4)
            )
            found = (
                (north_lead, south_lead),
                (north - north_lead + last, (south - south_lead + last) * turned),
            )
            for which, (north, south) in enumerate(found):
                if odd_slot:
                    both = jnp.where(low, pltpu.roll(north, LANES // 2, 1), south)
                else:
                    both = jnp.where(low, north, pltpu.roll(south, LANES // 2, 1))
                at = pl.multiple_of((2 * slot + which) * rows, rows)
                sums[pl.ds(at, rows), :] = jnp.take_along_axis(
                    both, lanes, axis=1, mode="promise_in_bounds"
                )
        return carry

    [combine(i, 0) for i in range(pairs)]

    waves = 2 * slots
    share = LANES // parts
    per = LANES // share
    group = iota((waves, LANES), 1) // share
    mine = pl.ds(pl.multiple_of(unit * waves, waves), waves)
    for part in range(2):
        for block in range(times // per):
            sources = []
            for place in range(per):
                step_of, member = (block * per + place) // members, (block * per + place) % members
                row = (member * steps + step_of) * 2 + part
                sources.append(sums[pl.ds(row, waves, stride=rows), :])
            for step in range(parts):
                built = sources[step]
                for place in range(1, per):
                    built = jnp.where(group == place, sources[place ^ step], built)
                outs[step][part, mine, block * LANES : (block + 1) * LANES] = built


def legendre_sums(spectra, turned, pair_of_slot, here, owner, first_unit, units, parts):
    members, steps, _, _, length = spectra.shape
    slots = 2 * PAIRS_UNIT
    waves = 2 * slots
    times = members * steps
    width = times * LANES // parts
    known = first_unit > 0
    out = [jax.ShapeDtypeStruct((2, units * waves, width), F32)] * parts
    if not known:
        out = out + [jax.ShapeDtypeStruct((2 * times, LANES), jnp.int32)]
    here_spec = pl.BlockSpec(memory_space=pltpu.VMEM)
    away = pl.BlockSpec(memory_space=pltpu.HBM)
    return pl.pallas_call(
        functools.partial(legendre_kernel, first_unit, units, parts, known),
        grid_spec=pltpu.PrefetchScalarGridSpec(
            num_scalar_prefetch=2,
            grid=(units,),
            in_specs=[pl.BlockSpec(owner.shape, lambda u, *_: (0, 0)), away, away],
            out_specs=[here_spec] * len(out),
            scratch_shapes=[
                pltpu.VMEM((2, members, steps, slots, 2, length), BF16),
                pltpu.VMEM((2, length, PAIRS_UNIT, LANES), BF16),
                pltpu.VMEM((PAIRS_UNIT, length - 1, LANES), BF16),
                pltpu.VMEM((PAIRS_UNIT, 16 * times, LANES), F32),
                pltpu.VMEM((waves * 2 * times, LANES), F32),
                pltpu.VMEM((PAIRS_UNIT, LANES), F32),
                pltpu.SemaphoreType.DMA((2,)),
                pltpu.SemaphoreType.DMA((2, CUTS)),
            ],
        ),
        out_shape=out,
        compiler_params=pltpu.CompilerParams(vmem_limit_bytes=LEGENDRE_VMEM),
        cost_estimate=pl.CostEstimate(
            flops=units * PAIRS_UNIT * 2 * LANES * LANES * length,
            bytes_accessed=units * PAIRS_UNIT * (LANES + 2 * 2 * times) * length * 2,
            transcendentals=0,
        ),
        name="legendre",
    )(pair_of_slot, here, owner, spectra, turned)


def split(x):
    high = x.astype(BF16)
    return high, (x - high.astype(F32)).astype(BF16)


def turns(numbers, full):
    quarter = full // 4
    turned = (numbers + quarter // 2) // quarter
    x = (numbers - turned * quarter).astype(F32) * (2.0 * math.pi / full)
    y = x * x
    sine = x * (1.0 + y * (-1 / 6 + y * (1 / 120 + y * (-1 / 5040 + y * (1 / 362880)))))
    cosine = 1.0 + y * (-1 / 2 + y * (1 / 24 + y * (-1 / 720 + y * (1 / 40320 - y * (1 / 3628800)))))
    odd = turned % 2 == 1
    c, s = jnp.where(odd, sine, cosine), jnp.where(odd, cosine, sine)
    c = jnp.where((turned == 1) | (turned == 2), -c, c)
    s = jnp.where((turned == 2) | (turned == 3), -s, s)
    return c, s


def regrouped(x, step, share):
    if step == 0:
        return x
    shape = (x.shape[0], LANES)
    index = lax.bitwise_xor(iota(shape, 1), jnp.int32(step * share))
    return jnp.concatenate(
        [
            jnp.take_along_axis(x[:, i : i + LANES], index, axis=1, mode="promise_in_bounds")
            for i in range(0, x.shape[1], LANES)
        ],
        axis=1,
    )


def tables_kernel(lon, top, waves_ref, coef_ref, t_cos_h, t_cos_l, t_sin_h, t_sin_l, base_ref):
    half, depth = t_cos_h.shape
    coarse = half // NB
    full = 8 * top
    waves = waves_ref[...]
    at = 0
    for factor, shift_by, count in ((2 * NB, 0, coarse), (2, 1, NB)):
        number = factor * iota((count, depth), 0) + shift_by
        c, s = turns(number * waves % full, full)
        base_ref[at : at + count, :] = c
        base_ref[at + count : at + 2 * count, :] = s
        at += 2 * count
    c, s = turns((lon - 1) * waves % full, full)
    rate = waves.astype(F32) * (1.0 / top)
    scale = top ** (-0.5)
    kind = iota((8, depth), 0)
    turn = jnp.where(kind == 0, c * scale, jnp.where(kind == 1, s * scale, rate))
    coef_ref[...] = turn.T

    def fill(a, carry):
        ca = base_ref[pl.ds(a, 1), :]
        sa = base_ref[pl.ds(coarse + a, 1), :]
        cb = base_ref[2 * coarse : 2 * coarse + NB, :]
        sb = base_ref[2 * coarse + NB : 2 * coarse + 2 * NB, :]
        at = pl.ds(pl.multiple_of(a * NB, NB), NB)
        t_cos_h[at, :], t_cos_l[at, :] = split(ca * cb - sa * sb)
        t_sin_h[at, :], t_sin_l[at, :] = split(sa * cb + ca * sb)
        return carry

    lax.fori_loop(0, coarse, fill, 0)


def tables(waves, lon, top):
    depth = waves.shape[1]
    held = pl.BlockSpec(memory_space=pltpu.VMEM)
    out = [jax.ShapeDtypeStruct((depth, 8), F32)]
    out += [jax.ShapeDtypeStruct((lon // 2, depth), BF16)] * 4
    return pl.pallas_call(
        functools.partial(tables_kernel, lon, top),
        in_specs=[held],
        out_specs=[held] * 5,
        out_shape=out,
        scratch_shapes=[pltpu.VMEM((2 * (lon // 2 // NB + NB), depth), F32)],
        compiler_params=pltpu.CompilerParams(vmem_limit_bytes=TABLES_VMEM),
        cost_estimate=pl.CostEstimate(
            flops=16 * lon * depth, bytes_accessed=4 * lon * depth, transcendentals=0
        ),
        name="tables",
    )(waves)


def synthesis_kernel(counts, fresh, closing, shape, *refs):
    lon, regions, wide, share = shape
    refs = list(refs)
    if closing:
        starts_ref, here_ref = refs.pop(0), refs.pop(0)
    coef_ref, *table_refs = [refs.pop(0) for _ in range(5)]
    pieces = [refs.pop(0) for _ in counts]
    if not fresh:
        cos_in, sin_in = refs.pop(0), refs.pop(0)
    if closing:
        outs = [refs.pop(0) for _ in range(wide)]
    else:
        cos_out, sin_out = refs.pop(0), refs.pop(0)
    w_cos_h, w_cos_l, w_sin_h, w_sin_l = refs[:4]
    step = pl.program_id(0)
    block = lon // 2 // pl.num_programs(0)
    width = pieces[0].shape[2]
    here_rows = pl.ds(pl.multiple_of(step * block, block), block)

    @pl.when(step == 0)
    def _():
        at = 0
        for piece, (count, step_of) in zip(pieces, counts):
            span = slice(at, at + count)
            coef = coef_ref[span, :]
            c, s, rate = coef[:, 0:1], coef[:, 1:2], coef[:, 2:3]
            real, imag = (regrouped(piece[i], step_of, share) for i in range(2))
            p0 = real * c - imag * s
            p1 = real * s + imag * c
            for index, value in enumerate((p0, rate * p1)):
                cols = slice(index * width, (index + 1) * width)
                w_cos_h[span, cols], w_cos_l[span, cols] = split(value)
            for index, value in enumerate((p1, rate * p0)):
                cols = slice(index * width, (index + 1) * width)
                w_sin_h[span, cols], w_sin_l[span, cols] = split(value)
            at += count

    t_cos_h, t_cos_l, t_sin_h, t_sin_l = (table.at[here_rows, :] for table in table_refs)

    def product(table_h, table_l, weight_h, weight_l):
        dot = functools.partial(jnp.dot, preferred_element_type=F32)
        return (
            dot(table_h[...], weight_h[...])
            + dot(table_l[...], weight_h[...])
            + dot(table_h[...], weight_l[...])
        )

    even = product(t_cos_h, t_cos_l, w_cos_h, w_cos_l)
    odd = product(t_sin_h, t_sin_l, w_sin_h, w_sin_l)
    if not fresh:
        even = even + cos_in[here_rows, :]
        odd = odd + sin_in[here_rows, :]
    if not closing:
        cos_out[here_rows, :] = even
        sin_out[here_rows, :] = odd
        return

    value_ref, slope_ref, found_v, found_s = refs[4:]
    half = lon // 2

    def narrowed(x):
        return functools.reduce(
            jnp.maximum, [x[:, i : i + LANES] for i in range(0, width, LANES)]
        )

    a, d = even[:, :width], even[:, width:]
    b, c = odd[:, :width], odd[:, width:]
    below = pl.ds(pl.multiple_of(step * block, block), block)
    above = pl.ds(pl.multiple_of(half + step * block, block), block)
    value_ref[below, :] = narrowed(a + b)
    value_ref[above, :] = narrowed(a - b)
    slope_ref[below, :] = narrowed(jnp.abs(c - d))
    slope_ref[above, :] = narrowed(jnp.abs(c + d))

    @pl.when(step == pl.num_programs(0) - 1)
    def _():
        window = (WIDEST_REGION + 15) // 8 * 8
        rows = iota((window, LANES), 0)

        def best(low, high):
            at = pl.multiple_of(jnp.minimum(low // 8 * 8, lon - window), 8)
            inside = (rows >= low - at) & (rows < high - at)
            v = jnp.where(inside, value_ref[pl.ds(at, window), :], -3e38)
            s = jnp.where(inside, slope_ref[pl.ds(at, window), :], -3e38)
            return jnp.max(v, axis=0, keepdims=True), jnp.max(s, axis=0, keepdims=True)

        def one(region, carry):
            begin, end = starts_ref[region], starts_ref[region + 1]
            upper = end > half
            low = jnp.where(upper, jnp.maximum(begin, half), half - end)
            high = jnp.where(upper, end, half - begin)
            v, s = best(low, high)
            found_v[pl.ds(region, 1), :] = v
            found_s[pl.ds(region, 1), :] = s
            return carry

        lax.fori_loop(0, regions, one, 0, unroll=8)
        centre = starts_ref[regions + 1]
        v, s = best(0, half - starts_ref[centre])
        at = pl.ds(centre, 1)
        found_v[at, :] = jnp.maximum(found_v[at, :], v)
        found_s[at, :] = jnp.maximum(found_s[at, :], s)
        values, slopes = found_v[...], found_s[...]
        span = LANES
        while span > LANES // 2:
            span //= 2
            values = jnp.maximum(values, pltpu.roll(values, span, 1))
            slopes = jnp.maximum(slopes, pltpu.roll(slopes, span, 1))
        found_v[...] = jnp.where(iota(values.shape, 1) < LANES // 2, values, slopes)
        for offset in range(wide):
            owner = lax.rem(here_ref[0] + offset, wide)
            start = pl.multiple_of(owner * REG_DEV, REG_DEV)
            outs[offset][...] = found_v[pl.ds(start, REG_DEV), :]


def synthesis(made, pieces, sources, held, closing, lon, regions, wide, share, starts, here):
    block = min(1024, lon // 2)
    depth = made[0].shape[0]
    counts = tuple((piece.shape[1], source) for piece, source in zip(pieces, sources))
    width = pieces[0].shape[2]
    fresh = held is None
    prefetch = (starts, here) if closing else ()
    operands = [*made, *pieces] + ([] if fresh else list(held))
    in_specs = [pl.BlockSpec(memory_space=pltpu.VMEM)] * len(operands)
    scratch = [pltpu.VMEM((depth, 2 * width), BF16)] * 4
    if closing:
        out_shape = [jax.ShapeDtypeStruct((REG_DEV, LANES), F32)] * wide
        scratch += [pltpu.VMEM((lon, LANES), F32)] * 2 + [pltpu.VMEM((regions, LANES), F32)] * 2
    else:
        out_shape = [jax.ShapeDtypeStruct((lon // 2, 2 * width), F32)] * 2
    out_specs = [pl.BlockSpec(memory_space=pltpu.VMEM)] * len(out_shape)
    return pl.pallas_call(
        functools.partial(
            synthesis_kernel, counts, fresh, closing, (lon, regions, wide, share)
        ),
        grid_spec=pltpu.PrefetchScalarGridSpec(
            num_scalar_prefetch=len(prefetch),
            grid=(lon // 2 // block,),
            in_specs=in_specs,
            out_specs=out_specs,
            scratch_shapes=scratch,
        ),
        out_shape=out_shape,
        compiler_params=pltpu.CompilerParams(vmem_limit_bytes=SYNTHESIS_VMEM),
        cost_estimate=pl.CostEstimate(
            flops=6 * depth * lon * 2 * width, bytes_accessed=16 * lon * width, transcendentals=0
        ),
        name="synthesis",
    )(*prefetch, *operands)


def shift(x, axis, count, step):
    return lax.ppermute(x, axis, [(i, (i + step) % count) for i in range(count)])


def swap(x, axis, count, step):
    return lax.ppermute(x, axis, [(i, i ^ step) for i in range(count)])


def final_kernel(*refs):
    *found, peak_ref, slope_ref = refs
    best = functools.reduce(jnp.maximum, [x[...] for x in found])
    members, _, share = peak_ref.shape
    for member in range(members):
        peak_ref[member] = best[:, member * share : (member + 1) * share]
        at = LANES // 2 + member * share
        slope_ref[member] = best[:, at : at + share]


def kernels(spectra, legendre, pair_of_slot, lat_owner, region_of_lon):
    members, steps, slot_count, _, length = spectra.shape
    top = length - 1
    lon = region_of_lon.shape[0]
    parts = lax.axis_size("narrow")
    wide = lax.axis_size("wide")
    regions = REG_DEV * wide
    here = lax.axis_index("narrow")
    here_wide = lax.axis_index("wide")
    here_ref = here.reshape(1)
    owner = lat_owner.reshape(1, -1)
    turned = jnp.transpose(legendre, (1, 0, 2))
    tied = lax.optimization_barrier

    kept, beside, near, far, first = [], [], [], [], 0
    for number, units in enumerate(CHUNKS):
        if number >= 1:
            here_ref, kept[-1] = tied((here_ref, kept[-1]))
        if number == 2:
            pair_here, region_of_lon, kept[-1] = tied((pair_of_slot, region_of_lon, kept[-1]))
        if number >= 2:
            here_ref, far[number - 2] = tied((here_ref, far[number - 2]))
        if number >= 3:
            ready = [g for g, group in enumerate(GROUPS) if group[-1] == number - 2]
            for g in ready:
                here_ref, near[g] = tied((here_ref, near[g]))
        sums = legendre_sums(
            spectra, turned, pair_of_slot, here_ref, owner, first, units, parts
        )
        if number == 0:
            owner = sums[parts]
        kept.append(sums[0])
        beside.append(sums[1])
        far.append([swap(sums[i], "narrow", parts, i) for i in range(2, parts)])
        for group in GROUPS:
            if group[-1] == number:
                near.append(swap(jnp.concatenate([beside[i] for i in group], axis=1), "narrow", parts, 1))
        first += units

    waves_of = jnp.stack([pair_here, top - 1 - pair_here], axis=1).reshape(parts, -1)
    waves_of = waves_of[lax.bitwise_xor(here, jnp.arange(parts, dtype=jnp.int32))]
    edges = jnp.arange(regions + 1, dtype=jnp.int32)
    starts = jnp.sum((region_of_lon[None, :] < edges[:, None]).astype(jnp.int32), axis=1)
    starts = jnp.concatenate([starts, region_of_lon[lon // 2 - 1 : lon // 2]])

    per_unit = 4 * PAIRS_UNIT
    bounds = [0]
    for units in CHUNKS:
        bounds.append(bounds[-1] + units * per_unit)

    def piece(array, source, chunks):
        return array, source, [waves_of[source, bounds[i] : bounds[i + 1]] for i in chunks]

    late = len(CHUNKS) - 1
    own = [piece(kept[i], 0, (i,)) for i in range(late + 1)]
    swapped = [piece(near[g], 1, group) for g, group in enumerate(GROUPS)]
    across = [
        [piece(array, 2 + i, (chunk,)) for i, array in enumerate(far[chunk])]
        for chunk in range(late + 1)
    ]
    stages = (
        own[:late] + swapped[:-1] + sum(across[:late], []),
        own[late:] + swapped[-1:] + across[late],
    )
    held = None
    waves = [jnp.concatenate([w for _, _, found in stage for w in found]) for stage in stages]
    made = [tables(w.reshape(1, -1), lon, top) for w in tied((*waves, kept[-1]))[:-1]]
    for number, stage in enumerate(stages):
        held = synthesis(
            made[number],
            [array for array, _, _ in stage],
            [source for _, source, _ in stage],
            held,
            number == len(stages) - 1,
            lon,
            regions,
            wide,
            LANES // parts,
            starts,
            here_wide.reshape(1),
        )

    found = [held[0]] + [shift(held[i], "wide", wide, i) for i in range(1, wide)]
    out = jax.ShapeDtypeStruct((members, REG_DEV, LANES // 2 // members), F32)
    peak, peak_slope = pl.pallas_call(
        final_kernel,
        in_specs=[pl.BlockSpec(memory_space=pltpu.VMEM)] * wide,
        out_shape=[out] * 2,
        compiler_params=pltpu.CompilerParams(vmem_limit_bytes=TABLES_VMEM),
        name="final",
    )(*found)
    return jnp.transpose(peak, (0, 2, 1)), jnp.transpose(peak_slope, (0, 2, 1))


def per_device(spectra, legendre, pair_of_slot, lat_owner, region_of_lon):
    members, steps, _, _, length = spectra.shape
    pairs, _, lanes = legendre.shape
    share = lat_owner.shape[0] // lax.axis_size("narrow")
    parts = lax.axis_size("narrow")
    fits = (
        parts & (parts - 1) == 0
        and pairs == PAIRS_UNIT * sum(CHUNKS)
        and lanes == LANES
        and lat_owner.shape[0] == LANES
        and 2 * members * share == LANES
        and members * steps * share % LANES == 0
        and (length - 1) % LANES == 0
        and region_of_lon.shape[0] % 1024 == 0
    )
    run = kernels if fits else plain
    return run(spectra, legendre, pair_of_slot, lat_owner, region_of_lon)


def solution(mesh):
    in_specs = (
        P(None, ("groups", "wide"), "narrow", None, None),
        P("narrow", None, None),
        P(),
        P(),
        P(),
    )
    out_specs = (P("groups", "narrow", "wide"), P("groups", "narrow", "wide"))
    return jax.shard_map(
        per_device, mesh=mesh, in_specs=in_specs, out_specs=out_specs, check_vma=False
    )
```
